512 devices in a mesh: section: 4 (over x), space: 128 (over z, y, core).
Axes of the slice: x: 4, y: 8, z: 8, core: 2. Of those that a mesh axis runs over, the one named last changes fastest.
Arguments:
- grid_inputs: bfloat16 [2, 65536, 474], P(None, ('section', 'space')), may hold values from -6 to 6
- embed_weight: bfloat16 [474, 512], replicated, may hold values from -0.25 to 0.25
- embed_bias: float32 [512], replicated, may hold values from -3 to 3
- encode_weight: bfloat16 [512, 512], replicated, may hold values from -0.25 to 0.25
- encode_edge_weight: float32 [4, 512], replicated, may hold values from -3 to 3
- encode_bias: float32 [512], replicated, may hold values from -3 to 3
- mesh_gain: float32 [512], replicated, may hold values from 0.1 to 1.9
- process_weight: bfloat16 [4, 4, 512, 512], P('section'), may hold values from -0.25 to 0.25
- process_edge_weight: float32 [4, 4, 512], P('section'), may hold values from -3 to 3
- process_bias: float32 [4, 2, 512], P('section'), may hold values from -3 to 3
- process_gain: float32 [4, 512], P('section'), may hold values from 0.1 to 1.9
- decode_weight: bfloat16 [2, 512, 512], replicated, may hold values from -0.25 to 0.25
- decode_edge_weight: float32 [4, 512], replicated, may hold values from -3 to 3
- decode_bias: float32 [512], replicated, may hold values from -3 to 3
- output_weight: bfloat16 [512, 227], replicated, may hold values from -0.25 to 0.25
- encode_senders: int32 [4, 128, 192], P('section', 'space'), may hold values from 0 to 127, as said below
- encode_receivers: int32 [4, 128, 192], P('section', 'space'), may hold values from 0 to 128, as said below
- encode_features: float32 [4, 4, 128, 192], P(None, 'section', 'space'), may hold values from -6 to 6
- halo_send_rows: int32 [128, 64], P('space'), may hold values from 0 to 127, as said below
- mesh_senders: int32 [128, 448], P('space'), may hold values from 0 to 319, as said below
- mesh_receivers: int32 [128, 448], P('space'), may hold values from 0 to 127, as said below
- mesh_features: float32 [4, 128, 448], P(None, 'space'), may hold values from -6 to 6
- decode_senders: int32 [4, 128, 192], P('section', 'space'), may hold values from 0 to 127, as said below
- decode_receivers: int32 [4, 128, 192], P('section', 'space'), may hold values from 0 to 128, as said below
- decode_features: float32 [4, 4, 128, 192], P(None, 'section', 'space'), may hold values from -6 to 6
Outputs:
- forecast: bfloat16 [2, 65536, 227], P(None, ('section', 'space'))
The draws below stay inside these ranges and needn't reach their ends.
Inputs may be any that keep to these rules, and one draw needn't show every extreme that they name: `encode_senders`: entry [s, q, i * 64 + k] is the local grid row that grid device (s, q) sends as its k-th row to mesh owner (s, (q + o_i) mod 128), o = (0, 1, -1). `encode_receivers`: entry [s, p, i * 64 + k] is the local mesh row of owner (s, p) that takes the k-th row from grid device (s, (p - o_i) mod 128); 128 marks an empty slot, used slots come first in each block of 64, and block 0 is full. `halo_send_rows`: entry [p, b * 16 + k] is the local mesh row that owner p sends to owner (p + h_b) mod 128 as its k-th halo row, h = (1, -1, 2, -2). `mesh_senders`: encoded as in the step on mesh edges; every value is used on every owner. `mesh_receivers`: the local mesh row that the edge updates; every row receives an edge. `decode_senders`: entry [s, p, i * 64 + k] is the local mesh row that owner (s, p) sends as its k-th row to grid device (s, (p + o_i) mod 128). `decode_receivers`: entry [s, q, i * 64 + k] is the local grid row of device (s, q) that takes the k-th row from mesh owner (s, (q - o_i) mod 128); 128 marks an empty slot, used slots come first in each block of 64, and block 0 is full.
All inputs are finite; a program needn't handle non-finite values.
Results may differ from the reference program's by a relative error of at most 0.018.
Values may be sent and summed in bfloat16 or wider, within the bound.
No kernel may reach another device: no remote copies, remote signals or barrier semaphores. Data moves between devices by JAX's collectives and lax.ppermute only.
A program may use at most 64 MiB of HBM per device.

```python
import jax
import jax.numpy as jnp
from jax import lax

D = 512
IN_F = 474
VARS = 227
EDGE_DIM = 4
SAMPLES = 2
G_DEV = 128
M_DEV = 128
CAP = 64
HCAP = 16
COARSE = 1
GRID = 65536
SLOTS = 192
MESH_EDGES = 448
N_SECTION = 4
N_SPACE = 128


def slot_lists(key, sentinel):
    shape = (N_SECTION, N_SPACE, 3 * CAP)
    row_key, count_key = jax.random.split(key)
    rows = jax.random.randint(row_key, shape, 0, sentinel)
    counts = jax.random.randint(count_key, (N_SECTION, N_SPACE, 3), 0, CAP + 1)
    counts = counts.at[:, :, 0].set(CAP)
    counts = counts.at[:, :, 2].set(jnp.minimum(counts[:, :, 2], CAP - 1))
    slot_ids = jnp.arange(3 * CAP)
    slot_block = slot_ids // CAP
    place = slot_ids % CAP
    used = place[None, None, :] < jnp.take(counts, slot_block, axis=2)
    first_low = (slot_block == 0) & (place == 0)
    first_high = (slot_block == 0) & (place == 1)
    rows = jnp.where(first_low[None, None, :], 0, rows)
    rows = jnp.where(first_high[None, None, :], sentinel - 1, rows)
    return jnp.where(used, rows, sentinel).astype(jnp.int32)


def bounded_rows(key, shape, limit):
    rows = jax.random.randint(key, shape, 0, limit)
    rows = rows.at[..., 0].set(0)
    rows = rows.at[..., 1].set(limit - 1)
    return rows.astype(jnp.int32)


def mesh_lists(key):
    key = jax.random.fold_in(key, 60)
    local_sources = M_DEV + 4 * HCAP
    coarse_count = N_SPACE * COARSE
    rest_count = 2 * M_DEV + 4 * HCAP
    coarse_rows = min(M_DEV // 2, coarse_count)
    open_rows = M_DEV - coarse_rows

    def one_owner(owner_key):
        keys = jax.random.split(owner_key, 5)
        send_rest = jnp.concatenate([jax.random.permutation(keys[0], local_sources).astype(jnp.int32), jax.random.randint(keys[1], (rest_count - local_sources,), 0, local_sources).astype(jnp.int32)])
        recv_rest = coarse_rows + jnp.concatenate([jax.random.permutation(keys[2], open_rows).astype(jnp.int32), jax.random.randint(keys[3], (rest_count - open_rows,), 0, open_rows).astype(jnp.int32)])
        coarse_ids = jnp.arange(coarse_count, dtype=jnp.int32)
        senders = jnp.concatenate([local_sources + coarse_ids, send_rest])
        receivers = jnp.concatenate([coarse_ids % coarse_rows, recv_rest.astype(jnp.int32)])
        order = jax.random.permutation(keys[4], senders.shape[0])
        return (senders[order].astype(jnp.int32), receivers[order].astype(jnp.int32))
    return jax.vmap(one_owner)(jax.random.split(key, N_SPACE))


def draw_encode_senders(key, part):
    key = jax.random.fold_in(key, 3)
    return bounded_rows(key, (N_SECTION, N_SPACE, 3 * CAP), G_DEV)


def draw_encode_receivers(key, part):
    key = jax.random.fold_in(key, 1)
    return slot_lists(key, M_DEV)


def draw_decode_senders(key, part):
    key = jax.random.fold_in(key, 4)
    return bounded_rows(key, (N_SECTION, N_SPACE, 3 * CAP), M_DEV)


def draw_decode_receivers(key, part):
    key = jax.random.fold_in(key, 2)
    return slot_lists(key, G_DEV)


def draw_halo_send_rows(key, part):
    key = jax.random.fold_in(key, 5)
    return bounded_rows(key, (N_SPACE, 4 * HCAP), M_DEV)


def draw_mesh_senders(key, part):
    senders, receivers = mesh_lists(key)
    return senders


def draw_mesh_receivers(key, part):
    senders, receivers = mesh_lists(key)
    return receivers


def level_of(key, dims, cuts, low, top_value):
    def one(axis_at, shards_of):
        steps = jax.random.uniform(jax.random.fold_in(jax.random.fold_in(key, 6), axis_at), (shards_of,), jnp.float32, low / len(cuts), top_value / len(cuts))
        return jnp.repeat(jnp.exp(steps), dims[axis_at] // shards_of).reshape((-1,) + (1,) * (len(dims) - axis_at - 1))

    loudness = one(*cuts[0])
    for cut in cuts[1:]:
        loudness = loudness * one(*cut)
    return loudness


def noise(key, extent, deviation, reach, pieces=(), held_as=jnp.bfloat16):
    factor_of = level_of(key, extent, pieces, -0.22, 0.18) if pieces else 1.0
    values = jax.random.normal(key, extent, jnp.float32) * deviation * factor_of
    return jnp.minimum(jnp.maximum(values, -reach), reach).astype(held_as)


def setup_inputs(seed: int = 0) -> dict:
    key_list = jax.random.split(jax.random.key(seed), 26)
    grid_inputs = noise(key_list[0], (SAMPLES, GRID, IN_F), 1.0, 6.0, ((1, 512),))
    embed_weight = noise(key_list[1], (IN_F, D), IN_F ** -0.5, 0.25)
    embed_bias = noise(key_list[2], (D,), 0.5, 3.0, (), jnp.float32)
    encode_weight = noise(key_list[3], (D, D), D ** -0.5, 0.25)
    encode_edge_weight = noise(key_list[4], (EDGE_DIM, D), 0.5, 3.0, (), jnp.float32)
    encode_bias = noise(key_list[5], (D,), 0.5, 3.0, (), jnp.float32)
    mesh_gain = jnp.clip(1.0 + 0.18 * jax.random.normal(key_list[6], (D,), jnp.float32), 0.1, 1.9)
    process_weight = noise(key_list[7], (N_SECTION, 4, D, D), D ** -0.5, 0.25, ((0, 4),))
    process_edge_weight = noise(key_list[8], (N_SECTION, EDGE_DIM, D), 0.5, 3.0, ((0, 4),), jnp.float32)
    process_bias = noise(key_list[9], (N_SECTION, 2, D), 0.5, 3.0, ((0, 4),), jnp.float32)
    process_gain = jnp.clip(1.0 + 0.18 * jax.random.normal(key_list[10], (N_SECTION, D), jnp.float32), 0.1, 1.9)
    decode_weight = noise(key_list[11], (2, D, D), D ** -0.5, 0.25)
    decode_edge_weight = noise(key_list[12], (EDGE_DIM, D), 0.5, 3.0, (), jnp.float32)
    decode_bias = noise(key_list[13], (D,), 0.5, 3.0, (), jnp.float32)
    output_weight = noise(key_list[14], (D, VARS), D ** -0.5, 0.25)
    encode_senders = draw_encode_senders(jax.random.fold_in(key_list[25], 71), 0)
    encode_receivers = draw_encode_receivers(jax.random.fold_in(key_list[25], 71), 0)
    encode_features = noise(key_list[17], (EDGE_DIM, N_SECTION, N_SPACE, SLOTS), 1.0, 6.0, ((1, 4), (2, 128)), jnp.float32)
    halo_send_rows = draw_halo_send_rows(jax.random.fold_in(key_list[25], 71), 0)
    mesh_senders = draw_mesh_senders(jax.random.fold_in(key_list[25], 71), 0)
    mesh_receivers = draw_mesh_receivers(jax.random.fold_in(key_list[25], 71), 0)
    mesh_features = noise(key_list[21], (EDGE_DIM, N_SPACE, MESH_EDGES), 1.0, 6.0, ((1, 128),), jnp.float32)
    decode_senders = draw_decode_senders(jax.random.fold_in(key_list[25], 71), 0)
    decode_receivers = draw_decode_receivers(jax.random.fold_in(key_list[25], 71), 0)
    decode_features = noise(key_list[24], (EDGE_DIM, N_SECTION, N_SPACE, SLOTS), 1.0, 6.0, ((1, 4), (2, 128)), jnp.float32)
    return dict(grid_inputs=grid_inputs, embed_weight=embed_weight, embed_bias=embed_bias, encode_weight=encode_weight, encode_edge_weight=encode_edge_weight, encode_bias=encode_bias, mesh_gain=mesh_gain, process_weight=process_weight, process_edge_weight=process_edge_weight, process_bias=process_bias, process_gain=process_gain, decode_weight=decode_weight, decode_edge_weight=decode_edge_weight, decode_bias=decode_bias, output_weight=output_weight, encode_senders=encode_senders, encode_receivers=encode_receivers, encode_features=encode_features, halo_send_rows=halo_send_rows, mesh_senders=mesh_senders, mesh_receivers=mesh_receivers, mesh_features=mesh_features, decode_senders=decode_senders, decode_receivers=decode_receivers, decode_features=decode_features)


link_offsets = (0, 1, -1)
halo_offsets = (1, -1, 2, -2)

def edge_term(features, weight):
    running = features[0][:, None] * weight[0][None, :]
    for component in range(1, features.shape[0]):
        running = running + features[component][:, None] * weight[component][None, :]
    return running

def layer_norm(values, scales):
    center = values - lax.optimization_barrier(jnp.mean(values, axis=-1, keepdims=True))
    spread = lax.optimization_barrier(jnp.mean(center * center, axis=-1, keepdims=True))
    return center * lax.rsqrt(spread + 1e-05) * scales

def process(mesh_state, weights, edge_bias, node_bias, scales, sources, targets, row_count):
    source_keys = jnp.dot(mesh_state, weights[0], preferred_element_type=jnp.float32).astype(jnp.bfloat16)
    target_keys = jnp.dot(mesh_state, weights[1], preferred_element_type=jnp.float32).astype(jnp.bfloat16)
    summed_in = source_keys[sources].astype(jnp.float32) + target_keys[targets].astype(jnp.float32) + edge_bias
    hidden = jax.nn.silu(summed_in).astype(jnp.bfloat16)
    node_in = jax.ops.segment_sum(hidden.astype(jnp.float32), targets, num_segments=row_count).astype(jnp.bfloat16)
    update = jax.nn.silu(jnp.dot(node_in, weights[2], preferred_element_type=jnp.float32) + jnp.dot(mesh_state, weights[3], preferred_element_type=jnp.float32) + node_bias)
    return (mesh_state.astype(jnp.float32) + layer_norm(update, scales)).astype(jnp.bfloat16)

def reference(grid_inputs, embed_weight, embed_bias, encode_weight, encode_edge_weight, encode_bias, mesh_gain, process_weight, process_edge_weight, process_bias, process_gain, decode_weight, decode_edge_weight, decode_bias, output_weight, encode_senders, encode_receivers, encode_features, halo_send_rows, mesh_senders, mesh_receivers, mesh_features, decode_senders, decode_receivers, decode_features):
    grid_total = G_DEV * N_SECTION * N_SPACE
    mesh_total = M_DEV * N_SPACE
    slot_count = 3 * CAP
    send_count = 4 * HCAP
    section_ids = jnp.arange(N_SECTION, dtype=jnp.int32)[:, None, None]
    space_ids = jnp.arange(N_SPACE, dtype=jnp.int32)[None, :, None]
    slot_ids = jnp.arange(slot_count, dtype=jnp.int32)[None, None, :]
    slot_block = slot_ids // CAP
    link_shift = jnp.array(link_offsets, dtype=jnp.int32)[slot_block]
    peer_ids = (space_ids - link_shift) % N_SPACE
    encode_source = ((section_ids * N_SPACE + peer_ids) * G_DEV + encode_senders[section_ids, peer_ids, slot_ids]).reshape(-1)
    encode_target = jnp.where(encode_receivers == M_DEV, mesh_total, space_ids * M_DEV + encode_receivers).reshape(-1).astype(jnp.int32)
    encode_edge = edge_term(encode_features.reshape(EDGE_DIM, -1), encode_edge_weight) + encode_bias
    decode_source = (peer_ids * M_DEV + decode_senders[section_ids, peer_ids, slot_ids]).reshape(-1)
    decode_target = jnp.where(decode_receivers == G_DEV, grid_total, (section_ids * N_SPACE + space_ids) * G_DEV + decode_receivers).reshape(-1).astype(jnp.int32)
    decode_clamped = jnp.minimum(decode_target, grid_total - 1)
    decode_edge = edge_term(decode_features.reshape(EDGE_DIM, -1), decode_edge_weight) + decode_bias
    owner_ids = jnp.arange(N_SPACE, dtype=jnp.int32)[:, None]
    source_index = mesh_senders
    halo_index = jnp.clip(source_index - M_DEV, 0, send_count - 1)
    halo_block = halo_index // HCAP
    halo_peer = (owner_ids - jnp.array(halo_offsets, dtype=jnp.int32)[halo_block]) % N_SPACE
    halo_row = halo_peer * M_DEV + halo_send_rows[halo_peer, halo_index]
    coarse_index = jnp.maximum(source_index - M_DEV - send_count, 0)
    coarse_row = coarse_index // COARSE * M_DEV + coarse_index % COARSE
    mesh_source = jnp.where(source_index < M_DEV, owner_ids * M_DEV + source_index, jnp.where(source_index < M_DEV + send_count, halo_row, coarse_row)).reshape(-1)
    mesh_target = (owner_ids * M_DEV + mesh_receivers).reshape(-1)
    mesh_feats = mesh_features.reshape(EDGE_DIM, -1)
    flat_in = grid_inputs.reshape(SAMPLES * grid_total, IN_F)
    grid_latent = jax.nn.silu(jnp.dot(flat_in, embed_weight, preferred_element_type=jnp.float32) + embed_bias).astype(jnp.bfloat16)
    grid_keys = jnp.dot(grid_latent, encode_weight, preferred_element_type=jnp.float32).astype(jnp.bfloat16)
    grid_keys = grid_keys.reshape(SAMPLES, grid_total, D)
    grid_queries = jnp.dot(grid_latent, decode_weight[1], preferred_element_type=jnp.float32).astype(jnp.bfloat16)
    grid_queries = grid_queries.reshape(SAMPLES, grid_total, D)
    results = []
    for sample in range(SAMPLES):
        message = jax.nn.silu(grid_keys[sample][encode_source].astype(jnp.float32) + encode_edge).astype(jnp.bfloat16)
        mesh_sum = jax.ops.segment_sum(message.astype(jnp.float32), encode_target, num_segments=mesh_total + 1)[:mesh_total]
        mesh_state = layer_norm(mesh_sum, mesh_gain).astype(jnp.bfloat16)
        for section_index in range(N_SECTION):
            edge_bias = edge_term(mesh_feats, process_edge_weight[section_index]) + process_bias[section_index, 0]
            mesh_state = process(mesh_state, process_weight[section_index], edge_bias, process_bias[section_index, 1], process_gain[section_index], mesh_source, mesh_target, mesh_total)
        mesh_keys = jnp.dot(mesh_state, decode_weight[0], preferred_element_type=jnp.float32).astype(jnp.bfloat16)
        summed_in = mesh_keys[decode_source].astype(jnp.float32) + grid_queries[sample][decode_clamped].astype(jnp.float32) + decode_edge
        hidden = jax.nn.silu(summed_in).astype(jnp.bfloat16)
        grid_sum = jax.ops.segment_sum(hidden.astype(jnp.float32), decode_target, num_segments=grid_total + 1)[:grid_total].astype(jnp.bfloat16)
        change = jnp.dot(grid_sum, output_weight, preferred_element_type=jnp.float32)
        results.append((grid_inputs[sample, :, :VARS].astype(jnp.float32) + change).astype(jnp.bfloat16))
    return jnp.stack(results)
```

```python
import functools

import jax
import jax.numpy as jnp
from jax import lax
from jax.experimental import pallas as pl
from jax.experimental.pallas import tpu as pltpu
from jax.sharding import PartitionSpec as P

BF = jnp.bfloat16
F32 = jnp.float32
ROWS = 128
HALO = 16
EXTRA = 64
NODE_BIAS, GAIN = 32, 35
VMEM_LIMIT = 24 * 1024 * 1024


def silu(v):
    return v * (0.5 + 0.5 * jnp.tanh(0.5 * v))


def dot(a, b):
    return jnp.dot(a, b, preferred_element_type=F32)


def dot_t(a, b):
    return lax.dot_general(a, b, (((0,), (0,)), ((), ())), preferred_element_type=F32)


def split3(x):
    hi = x.astype(BF)
    rest = x - hi.astype(F32)
    mid = rest.astype(BF)
    low = (rest - mid.astype(F32)).astype(BF)
    return hi, mid, low


def layer_norm(values, gain):
    center = values - jnp.mean(values, axis=-1, keepdims=True)
    spread = jnp.mean(center * center, axis=-1, keepdims=True)
    return center * lax.rsqrt(spread + 1e-05) * gain


def hot_rows(index_row, count):
    n = index_row.shape[1]
    return (lax.broadcasted_iota(jnp.int32, (count, n), 0) == index_row).astype(F32).astype(BF)


def feature_parts(features):
    hi, mid, low = split3(features)
    return jnp.concatenate([p.astype(F32) for p in (hi, hi, mid, mid, hi, low)], axis=0)


def weight_parts(weight):
    hi, mid, low = split3(weight)
    return jnp.concatenate([p.astype(F32) for p in (hi, mid, hi, mid, low, hi)], axis=0)


def edge_term(features, weight):
    return dot_t(feature_parts(features).astype(BF), weight_parts(weight).astype(BF))


def call(kernel, out, *args, smem=0, hbm=0, scratch=(), hbm_out=False, cost=1_000_000):
    count = len(args)
    specs = []
    for position in range(count):
        if position < smem:
            specs.append(pl.BlockSpec(memory_space=pltpu.SMEM))
        elif position >= count - hbm:
            specs.append(pl.BlockSpec(memory_space=pl.ANY))
        else:
            specs.append(pl.BlockSpec(memory_space=pltpu.VMEM))
    out_spec = pl.BlockSpec(memory_space=pl.ANY if hbm_out else pltpu.VMEM)
    return pl.pallas_call(
        kernel,
        out_shape=out,
        in_specs=specs,
        out_specs=jax.tree.map(lambda _: out_spec, out),
        scratch_shapes=list(scratch),
        compiler_params=pltpu.CompilerParams(vmem_limit_bytes=VMEM_LIMIT),
        cost_estimate=pl.CostEstimate(flops=cost, bytes_accessed=1_000_000, transcendentals=0),
    )(*args)


def shape(dims, dtype=BF):
    return jax.ShapeDtypeStruct(dims, dtype)


def pack_weights_kernel(core, edge_weight, bias, gain, weight, out, extras, sems):
    half = 2 * weight.shape[1]
    first = [
        pltpu.make_async_copy(
            weight.at[2 * core[0] + m],
            out.at[pl.ds(m * (half // 2), half // 2)],
            sems.at[m],
        )
        for m in range(2)
    ]
    for copy in first:
        copy.start()
    width = edge_weight.shape[1]
    b_parts = [p.astype(F32) for p in split3(bias[0:1, :])]
    n_parts = [p.astype(F32) for p in split3(bias[1:2, :])]
    g_parts = [p.astype(F32) for p in split3(gain[...])]
    rows = jnp.concatenate(
        [weight_parts(edge_weight[...])]
        + b_parts
        + [jnp.zeros((5, width), F32)]
        + n_parts
        + g_parts
        + [jnp.zeros((EXTRA - 38, width), F32)],
        axis=0,
    )
    extras[...] = rows.astype(BF)
    tail = pltpu.make_async_copy(extras, out.at[pl.ds(half, EXTRA)], sems.at[2])
    tail.start()
    for copy in first:
        copy.wait()
    tail.wait()


def setup_kernel(meta, edges_out, sums_out, halo_out, *, coarse):
    edges = sums_out.shape[2]
    padded = -(-edges // 128) * 128
    table = edges_out.shape[2]
    target_at = ROWS + 4 * HALO + coarse
    extra_at = target_at + ROWS
    for owner in range(2):
        senders = meta[owner, 0:1, :].astype(jnp.int32)
        receivers = meta[owner, 1:2, :].astype(jnp.int32)
        pad = padded - edges
        features = meta[owner, 4:8, :]
        if pad:
            senders = jnp.concatenate([senders, jnp.full((1, pad), -1, jnp.int32)], axis=1)
            receivers_wide = jnp.concatenate([receivers, jnp.full((1, pad), -1000, jnp.int32)], axis=1)
            features = jnp.concatenate([features, jnp.zeros((4, pad), F32)], axis=1)
        else:
            receivers_wide = receivers
        row = lax.broadcasted_iota(jnp.int32, (extra_at, padded), 0)
        hot = ((row == senders) | (row == receivers_wide + target_at)).astype(F32)
        tail = jnp.concatenate(
            [
                feature_parts(features),
                jnp.ones((3, padded), F32),
                jnp.zeros((EXTRA - 27, padded), F32),
            ],
            axis=0,
        )
        whole = jnp.concatenate([hot, tail], axis=0)
        edges_out[owner] = jnp.transpose(whole)[:edges].astype(BF)
        sums_out[owner] = hot_rows(receivers, ROWS)
    sent = (meta[0, 2:3, 0 : 8 * HALO] + meta[1, 2:3, 0 : 8 * HALO]).astype(jnp.int32)
    hot = (lax.broadcasted_iota(jnp.int32, (2 * ROWS, 8 * HALO), 0) == sent).astype(F32)
    halo_out[...] = jnp.transpose(hot).astype(BF)


def embed_kernel(core, x, embed_weight, embed_bias, encode_weight, query_weight, senders, own, near, far, queries):
    latent = silu(dot(x[...], embed_weight[...]) + embed_bias[...]).astype(BF)
    keys = dot(latent, encode_weight[...]).astype(BF)
    send_blocks(core, keys, senders, own, near, far)
    queries[...] = dot(latent, query_weight[...]).astype(BF)


def send_blocks(core, keys, senders, own, near, far):
    first = core[0] == 0
    cap = senders.shape[1] // 3
    hot = hot_rows(senders[...], ROWS)
    for sample in range(2):
        rows = dot_t(hot, keys[sample * ROWS : (sample + 1) * ROWS]).astype(BF)
        out = pl.ds(sample * cap, cap)
        own[out] = rows[:cap]
        near[out] = jnp.where(first, rows[cap : 2 * cap], rows[2 * cap :])
        far[out] = jnp.where(first, rows[2 * cap :], rows[cap : 2 * cap])


def arrived_rows(core, own, near, far, sample):
    first = core[0] == 0
    cap = own.shape[0] // 2
    at = pl.ds(sample * cap, cap)
    from_near = jnp.where(first, near[1, at], near[0, at])
    from_far = far[at]
    return jnp.concatenate(
        [own[at], jnp.where(first, from_far, from_near), jnp.where(first, from_near, from_far)],
        axis=0,
    ).astype(F32)


def message_kernel(core, own, near, far, features, weight, bias, receivers, out):
    edge = edge_term(features[...], weight[...]) + bias[...]
    hot = hot_rows(receivers[...], ROWS)
    for sample in range(2):
        rows = arrived_rows(core, own, near, far, sample)
        message = silu(rows + edge).astype(BF)
        sums = dot(hot, message).astype(BF)
        out[sample] = sums
        out[sample + 2] = sums


def start_kernel(parts, gain, out):
    total = parts[0].astype(F32)
    for section in range(1, parts.shape[0]):
        total = total + parts[section].astype(F32)
    out[...] = layer_norm(total, gain[...]).astype(BF)


def outgoing(core, state, halo_hot, coarse_out, halo_out, inner_out):
    rows = dot(halo_hot[...], state).astype(BF)
    halo_out[...] = jnp.where(core[0] == 0, rows[3 * HALO : 6 * HALO], rows[: 3 * HALO])
    inner_out[...] = rows[6 * HALO :]
    pair = jnp.concatenate([state[0:1].astype(F32), state[ROWS : ROWS + 1].astype(F32)], axis=0)
    coarse_out[...] = jnp.broadcast_to(pair.astype(BF)[None], coarse_out.shape)


def prepare_kernel(core, state, halo_hot, coarse_out, halo_out, inner_out):
    outgoing(core, state[...], halo_hot, coarse_out, halo_out, inner_out)


def layer_body(state, halo, inner, coarse, edges_hot, sums_hot, wbuf, ebuf, sources, table, waits):
    coarse_rows = coarse.shape[0]
    at_halo = 2 * ROWS
    at_inner = at_halo + 6 * HALO
    at_coarse = at_inner + 2 * HALO
    sources[0:at_halo] = state[...]
    sources[at_halo : at_halo + 3 * HALO] = halo[0]
    sources[at_halo + 3 * HALO : at_inner] = halo[1]
    sources[at_inner:at_coarse] = inner[...]
    sources[at_coarse : at_coarse + coarse_rows] = coarse[...]
    waits[0].wait()
    keys = dot(sources[...], wbuf[0]).astype(BF)
    waits[1].wait()
    target = dot(state[...], wbuf[1]).astype(BF)
    up, down = at_halo, at_halo + 3 * HALO
    halo_from = (
        (up + HALO, at_inner, up, down + HALO),
        (at_inner + HALO, down, up + 2 * HALO, down + 2 * HALO),
    )
    at_target = ROWS + 4 * HALO + coarse_rows
    waits[4].wait()
    nodes = []
    for owner in range(2):
        table[0:ROWS] = keys[owner * ROWS : (owner + 1) * ROWS]
        for block in range(4):
            source = halo_from[owner][block]
            table[ROWS + block * HALO : ROWS + (block + 1) * HALO] = keys[source : source + HALO]
        table[ROWS + 4 * HALO : at_target] = keys[at_coarse : at_coarse + coarse_rows]
        table[at_target : at_target + ROWS] = target[owner * ROWS : (owner + 1) * ROWS]
        table[at_target + ROWS :] = ebuf[...]
        hidden = silu(dot(edges_hot[owner], table[...])).astype(BF)
        nodes.append(dot(sums_hot[owner], hidden).astype(BF))
    node_in = jnp.concatenate(nodes, axis=0)
    waits[2].wait()
    waits[3].wait()

    def vector(at):
        return (ebuf[at : at + 1].astype(F32) + ebuf[at + 1 : at + 2].astype(F32)) + ebuf[
            at + 2 : at + 3
        ].astype(F32)

    update = silu(dot(node_in, wbuf[2]) + dot(state[...], wbuf[3]) + vector(NODE_BIAS))
    return (state[...].astype(F32) + layer_norm(update, vector(GAIN))).astype(BF)


def fetch(core, wbuf, ebuf, sems, mine, other, use_own=None, own=None, own_half=None):
    size = wbuf.shape[1]

    def from_half(half, m):
        return half.at[pl.ds((m % 2) * size, size)]

    got = None if use_own is None else jnp.logical_not(use_own)

    def both(condition):
        return condition if got is None else jnp.logical_and(got, condition)

    waits = []
    for m in range(4):
        if use_own is not None:

            @pl.when(use_own)
            def _(m=m):
                pltpu.make_async_copy(own.at[m], wbuf.at[m], sems.at[m]).start()

        @pl.when(both(core[0] == m // 2))
        def _(m=m):
            pltpu.make_async_copy(from_half(mine, m), wbuf.at[m], sems.at[m]).start()

        @pl.when(both(core[0] != m // 2))
        def _(m=m):
            pltpu.make_async_copy(from_half(other, m), wbuf.at[m], sems.at[m]).start()

        waits.append(pltpu.make_async_copy(from_half(mine, m), wbuf.at[m], sems.at[m]))
    tail = pl.ds(2 * size, EXTRA)
    if use_own is not None:

        @pl.when(use_own)
        def _():
            pltpu.make_async_copy(own_half.at[tail], ebuf, sems.at[4]).start()

        @pl.when(got)
        def _():
            pltpu.make_async_copy(mine.at[tail], ebuf, sems.at[4]).start()

    else:
        pltpu.make_async_copy(mine.at[tail], ebuf, sems.at[4]).start()
    waits.append(pltpu.make_async_copy(mine.at[tail], ebuf, sems.at[4]))
    return waits


def early_layer_kernel(
    core, state, halo, inner, coarse, edges_hot, sums_hot, halo_hot, own, own_half, mine, other,
    state_out, coarse_out, halo_out, inner_out, wbuf, ebuf, sources, table, sems, *, layer,
):
    waits = fetch(core, wbuf, ebuf, sems, mine, other, core[1] == layer, own, own_half)
    new = layer_body(state, halo, inner, coarse, edges_hot, sums_hot, wbuf, ebuf, sources, table, waits)
    state_out[...] = new
    outgoing(core, new, halo_hot, coarse_out, halo_out, inner_out)


def late_layer_kernel(
    core, state, halo, inner, coarse, edges_hot, sums_hot, halo_hot, mine, other,
    state_out, coarse_out, halo_out, inner_out, wbuf, ebuf, sources, table, sems, *, layer,
):
    waits = fetch(core, wbuf, ebuf, sems, mine.at[layer], other.at[layer - 2])
    new = layer_body(state, halo, inner, coarse, edges_hot, sums_hot, wbuf, ebuf, sources, table, waits)
    state_out[...] = new
    outgoing(core, new, halo_hot, coarse_out, halo_out, inner_out)


def last_layer_kernel(
    core, state, halo, inner, coarse, edges_hot, sums_hot, decode, mine, other,
    keys_out, wbuf, ebuf, sources, table, sems, *, layer,
):
    waits = fetch(core, wbuf, ebuf, sems, mine.at[layer], other.at[layer - 2])
    new = layer_body(state, halo, inner, coarse, edges_hot, sums_hot, wbuf, ebuf, sources, table, waits)
    own = jnp.where(core[0] == 0, new[:ROWS], new[ROWS:])
    keys = dot(own, decode[...]).astype(BF)
    for section in range(keys_out.shape[0]):
        keys_out[section] = keys


def deliver_kernel(core, keys, senders, own, near, far):
    both = jnp.concatenate([keys[0], keys[1]], axis=0)
    send_blocks(core, both, senders, own, near, far)


def decode_kernel(core, own, near, far, queries, features, weight, bias, receivers, x, out_weight, out):
    edge = edge_term(features[...], weight[...]) + bias[...]
    hot = hot_rows(receivers[...], ROWS)
    width = out_weight.shape[1]
    for sample in range(2):
        at = pl.ds(sample * ROWS, ROWS)
        rows = arrived_rows(core, own, near, far, sample)
        hidden = silu(rows + dot_t(hot, queries[at]) + edge).astype(BF)
        total = dot(hot, hidden).astype(BF)
        change = dot(total, out_weight[...])
        out[sample] = (x[at, :width].astype(F32) + change).astype(BF)


def shards(
    grid_inputs, embed_weight, embed_bias, encode_weight, encode_edge_weight, encode_bias, mesh_gain,
    process_weight, process_edge_weight, process_bias, process_gain, decode_weight, decode_edge_weight,
    decode_bias, output_weight, encode_senders, encode_receivers, encode_features, halo_send_rows,
    mesh_senders, mesh_receivers, mesh_features, decode_senders, decode_receivers, decode_features,
):
    samples, grid_rows, in_width = grid_inputs.shape
    latent = embed_weight.shape[1]
    owners = lax.axis_size("space")
    chips = owners // 2
    sections = lax.axis_size("section")
    section = lax.axis_index("section")
    core_id = lax.axis_index("space") % 2
    core = jnp.stack([core_id, section % 2]).astype(jnp.int32)
    pairs = [[2 * k, 2 * k + 1] for k in range(chips)]
    same_core = [[2 * k + c for k in range(chips)] for c in range(2)]
    to_neighbour = [(2 * k + 1, (2 * k + 2) % owners) for k in range(chips)] + [
        (2 * k, (2 * k - 1) % owners) for k in range(chips)
    ]
    swap = [(i, i ^ 1) for i in range(owners)]

    def gather_pair(value):
        return lax.all_gather(value, "space", axis=0, axis_index_groups=pairs)

    def to_next(value):
        return lax.ppermute(value, "space", to_neighbour)

    def vec(value):
        return value.reshape(1, -1)

    half_rows = 2 * latent + EXTRA
    half = call(
        pack_weights_kernel,
        shape((half_rows, latent)),
        core, process_edge_weight[0], process_bias[0], process_gain, process_weight[0],
        smem=1, hbm=1, hbm_out=True,
        scratch=[pltpu.VMEM((EXTRA, latent), BF), pltpu.SemaphoreType.DMA((3,))],
    )
    partner = lax.ppermute(half, "section", [(i, i ^ 1) for i in range(sections)])

    x = grid_inputs.reshape(samples * grid_rows, in_width)
    cap = encode_senders.shape[2] // 3
    block = shape((samples * cap, latent))
    own, near, far, queries = call(
        embed_kernel,
        (block, block, block, shape((samples * grid_rows, latent))),
        core, x, embed_weight, vec(embed_bias), encode_weight, decode_weight[1], encode_senders[0],
        smem=1,
    )
    far = to_next(far)
    near = gather_pair(near)
    edges = mesh_senders.shape[1]
    b = halo_send_rows.reshape(4, HALO)
    none = jnp.zeros((HALO,), jnp.int32)
    low = jnp.concatenate([b[2], none, none, b[1], b[3], none, none, b[0]])
    high = jnp.concatenate([none, b[0] + ROWS, b[2] + ROWS, none, none, b[3] + ROWS, b[1] + ROWS, none])
    halo_list = jnp.pad(jnp.where(core_id == 0, low, high), (0, edges - 8 * HALO))
    meta = jnp.concatenate(
        [
            jnp.stack([mesh_senders[0], mesh_receivers[0], halo_list, jnp.zeros_like(halo_list)]).astype(F32),
            mesh_features[:, 0, :],
        ],
        axis=0,
    )
    meta = gather_pair(meta)
    table_rows = 2 * ROWS + 4 * HALO + owners + EXTRA
    edges_hot, sums_hot, halo_hot = call(
        functools.partial(setup_kernel, coarse=owners),
        (shape((2, edges, table_rows)), shape((2, ROWS, edges)), shape((8 * HALO, 2 * ROWS))),
        meta,
    )
    parts = call(
        message_kernel,
        shape((sections, ROWS, latent)),
        core, own, near, far, encode_features[:, 0, 0, :], encode_edge_weight, vec(encode_bias), encode_receivers[0],
        smem=1,
    )
    parts = lax.all_to_all(parts, "section", 0, 0, tiled=True)
    start = call(start_kernel, shape((ROWS, latent)), parts, vec(mesh_gain))
    state = gather_pair(start).reshape(2 * ROWS, latent)

    partner_other = lax.ppermute(partner, "space", swap)
    sent_half = lax.optimization_barrier((half, partner))[0]
    gathered = lax.all_gather(sent_half, "section", axis=0)
    gathered_other = lax.ppermute(gathered[2:], "space", swap)

    outgoing_shapes = (
        shape((chips, 2, latent)),
        shape((3 * HALO, latent)),
        shape((2 * HALO, latent)),
    )
    scratch = [
        pltpu.VMEM((4, latent, latent), BF),
        pltpu.VMEM((EXTRA, latent), BF),
        pltpu.VMEM((2 * ROWS + 8 * HALO + owners, latent), BF),
        pltpu.VMEM((table_rows, latent), BF),
        pltpu.SemaphoreType.DMA((5,)),
    ]
    coarse, halo, inner = call(prepare_kernel, outgoing_shapes, core, state, halo_hot, smem=1)
    for layer in range(4):
        coarse = lax.all_to_all(coarse, "space", 0, 0, tiled=True, axis_index_groups=same_core)
        coarse = coarse.reshape(owners, latent)
        halo = gather_pair(to_next(halo))
        inputs = (core, state, halo, inner, coarse, edges_hot, sums_hot)
        if layer < 2:
            state, coarse, halo, inner = call(
                functools.partial(early_layer_kernel, layer=layer),
                (shape(state.shape),) + outgoing_shapes,
                *inputs, halo_hot, process_weight[0], half, partner, partner_other,
                smem=1, hbm=4, scratch=scratch,
            )
        elif layer < 3:
            state, coarse, halo, inner = call(
                functools.partial(late_layer_kernel, layer=layer),
                (shape(state.shape),) + outgoing_shapes,
                *inputs, halo_hot, gathered, gathered_other,
                smem=1, hbm=2, scratch=scratch,
            )
        else:
            keys = call(
                functools.partial(last_layer_kernel, layer=layer),
                shape((sections, ROWS, latent)),
                *inputs, decode_weight[0], gathered, gathered_other,
                smem=1, hbm=2, scratch=scratch,
            )

    keys = lax.all_to_all(keys, "section", 0, 0, tiled=True)
    own, near, far = call(deliver_kernel, (block, block, block), core, keys, decode_senders[0], smem=1)
    far = to_next(far)
    near = gather_pair(near)
    return call(
        decode_kernel,
        shape((samples, grid_rows, output_weight.shape[1])),
        core, own, near, far, queries, decode_features[:, 0, 0, :], decode_edge_weight, vec(decode_bias),
        decode_receivers[0], x, output_weight,
        smem=1,
    )


def solution(mesh):
    return jax.shard_map(
        shards,
        mesh=mesh,
        in_specs=(
            P(None, ("section", "space"), None),
            P(),
            P(),
            P(),
            P(),
            P(),
            P(),
            P("section", None, None, None),
            P("section", None, None),
            P("section", None, None),
            P("section", None),
            P(),
            P(),
            P(),
            P(),
            P("section", "space", None),
            P("section", "space", None),
            P(None, "section", "space", None),
            P("space", None),
            P("space", None),
            P("space", None),
            P(None, "space", None),
            P("section", "space", None),
            P("section", "space", None),
            P(None, "section", "space", None),
        ),
        out_specs=P(None, ("section", "space"), None),
        check_vma=False,
    )
```

```python
import functools

import jax
import jax.numpy as jnp
from jax import lax
from jax.experimental import pallas as pl
from jax.experimental.pallas import tpu as pltpu
from jax.sharding import PartitionSpec as P

BF = jnp.bfloat16
F32 = jnp.float32
ROWS = 128
HALO = 16
EXTRA = 64
NODE_BIAS, GAIN = 32, 35
SMALL_LIMIT = 16 * 1024 * 1024
LAYER_LIMIT = 63_000_000


def silu(v):
    return v * (0.5 + 0.5 * jnp.tanh(0.5 * v))


def dot(a, b):
    return jnp.dot(a, b, preferred_element_type=F32)


def dot_t(a, b):
    return lax.dot_general(a, b, (((0,), (0,)), ((), ())), preferred_element_type=F32)


def split3(x):
    hi = x.astype(BF)
    rest = x - hi.astype(F32)
    mid = rest.astype(BF)
    low = (rest - mid.astype(F32)).astype(BF)
    return hi, mid, low


def layer_norm(values, gain):
    center = values - jnp.mean(values, axis=-1, keepdims=True)
    spread = jnp.mean(center * center, axis=-1, keepdims=True)
    return center * lax.rsqrt(spread + 1e-05) * gain


def hot_rows(index_row, count):
    n = index_row.shape[1]
    return (lax.broadcasted_iota(jnp.int32, (count, n), 0) == index_row).astype(F32).astype(BF)


def feature_parts(features):
    hi, mid, low = split3(features)
    return jnp.concatenate([p.astype(F32) for p in (hi, hi, mid, mid, hi, low)], axis=0)


def weight_parts(weight):
    hi, mid, low = split3(weight)
    return jnp.concatenate([p.astype(F32) for p in (hi, mid, hi, mid, low, hi)], axis=0)


def edge_term(features, weight):
    return dot_t(feature_parts(features).astype(BF), weight_parts(weight).astype(BF))


def call(kernel, out, *args, smem=0, hbm=0, scratch=(), hbm_out=False, limit=SMALL_LIMIT):
    count = len(args)
    specs = []
    for position in range(count):
        if position < smem:
            specs.append(pl.BlockSpec(memory_space=pltpu.SMEM))
        elif position >= count - hbm:
            specs.append(pl.BlockSpec(memory_space=pltpu.HBM))
        else:
            specs.append(pl.BlockSpec(memory_space=pltpu.VMEM))
    out_spec = pl.BlockSpec(memory_space=pltpu.HBM if hbm_out else pltpu.VMEM)
    return pl.pallas_call(
        kernel,
        out_shape=out,
        in_specs=specs,
        out_specs=jax.tree.map(lambda _: out_spec, out),
        scratch_shapes=list(scratch),
        compiler_params=pltpu.CompilerParams(vmem_limit_bytes=limit),
        cost_estimate=pl.CostEstimate(flops=1_000_000, bytes_accessed=1_000_000, transcendentals=0),
    )(*args)


def shape(dims, dtype=BF):
    return jax.ShapeDtypeStruct(dims, dtype)


def pack_weights_kernel(core, edge_from, bias_from, gain_from, weight, out, edge_weight, bias, gain, packed, sems):
    size = weight.shape[1]
    half = 2 * size
    vectors = [
        pltpu.make_async_copy(source, target, sems.at[2 + i])
        for i, (source, target) in enumerate(
            ((edge_from, edge_weight), (bias_from, bias), (gain_from, gain))
        )
    ]
    matrices = [
        pltpu.make_async_copy(
            weight.at[2 * core[0] + m], packed.at[pl.ds(m * size, size)], sems.at[m]
        )
        for m in range(2)
    ]
    for copy in vectors + matrices:
        copy.start()
    for copy in vectors:
        copy.wait()
    width = edge_weight.shape[1]
    b_parts = [p.astype(F32) for p in split3(bias[0:1, :])]
    n_parts = [p.astype(F32) for p in split3(bias[1:2, :])]
    g_parts = [p.astype(F32) for p in split3(gain[...])]
    rows = jnp.concatenate(
        [weight_parts(edge_weight[...])]
        + b_parts
        + [jnp.zeros((5, width), F32)]
        + n_parts
        + g_parts
        + [jnp.zeros((EXTRA - 38, width), F32)],
        axis=0,
    )
    packed[half:] = rows.astype(BF)
    for copy in matrices:
        copy.wait()
    whole = pltpu.make_async_copy(packed, out, sems.at[0])
    whole.start()
    whole.wait()


def setup_kernel(meta, edges_out, sums_out, halo_out, *, coarse):
    edges = sums_out.shape[2]
    padded = -(-edges // 128) * 128
    table = edges_out.shape[2]
    target_at = ROWS + 4 * HALO + coarse
    extra_at = target_at + ROWS
    for owner in range(2):
        senders = meta[owner, 0:1, :].astype(jnp.int32)
        receivers = meta[owner, 1:2, :].astype(jnp.int32)
        pad = padded - edges
        features = meta[owner, 4:8, :]
        if pad:
            senders = jnp.concatenate([senders, jnp.full((1, pad), -1, jnp.int32)], axis=1)
            receivers_wide = jnp.concatenate([receivers, jnp.full((1, pad), -1000, jnp.int32)], axis=1)
            features = jnp.concatenate([features, jnp.zeros((4, pad), F32)], axis=1)
        else:
            receivers_wide = receivers
        row = lax.broadcasted_iota(jnp.int32, (extra_at, padded), 0)
        hot = ((row == senders) | (row == receivers_wide + target_at)).astype(F32)
        tail = jnp.concatenate(
            [
                feature_parts(features),
                jnp.ones((3, padded), F32),
                jnp.zeros((EXTRA - 27, padded), F32),
            ],
            axis=0,
        )
        whole = jnp.concatenate([hot, tail], axis=0)
        edges_out[owner] = jnp.transpose(whole)[:edges].astype(BF)
        sums_out[owner] = hot_rows(receivers, ROWS)
    sent = (meta[0, 2:3, 0 : 8 * HALO] + meta[1, 2:3, 0 : 8 * HALO]).astype(jnp.int32)
    hot = (lax.broadcasted_iota(jnp.int32, (2 * ROWS, 8 * HALO), 0) == sent).astype(F32)
    halo_out[...] = jnp.transpose(hot).astype(BF)


def embed_kernel(core, x, embed_weight, embed_bias, encode_weight, query_weight, senders, own, near, far, queries):
    latent = silu(dot(x[...], embed_weight[...]) + embed_bias[...]).astype(BF)
    keys = dot(latent, encode_weight[...]).astype(BF)
    send_blocks(core, keys, senders, own, near, far)
    queries[...] = dot(latent, query_weight[1]).astype(BF)


def send_blocks(core, keys, senders, own, near, far):
    first = core[0] == 0
    cap = senders.shape[1] // 3
    hot = hot_rows(senders[...], ROWS)
    for sample in range(2):
        rows = dot_t(hot, keys[sample * ROWS : (sample + 1) * ROWS]).astype(BF)
        out = pl.ds(sample * cap, cap)
        own[out] = rows[:cap]
        near[out] = jnp.where(first, rows[cap : 2 * cap], rows[2 * cap :])
        far[out] = jnp.where(first, rows[2 * cap :], rows[cap : 2 * cap])


def arrived_rows(core, own, near, far, sample):
    first = core[0] == 0
    cap = own.shape[0] // 2
    at = pl.ds(sample * cap, cap)
    from_near = jnp.where(first, near[1, at], near[0, at])
    from_far = jnp.where(first, far[0, at], far[1, at])
    return jnp.concatenate(
        [own[at], jnp.where(first, from_far, from_near), jnp.where(first, from_near, from_far)],
        axis=0,
    ).astype(F32)


def message_kernel(core, own, near, far, features, weight, bias, receivers, out):
    edge = edge_term(features[...], weight[...]) + bias[...]
    hot = hot_rows(receivers[...], ROWS)
    for sample in range(2):
        rows = arrived_rows(core, own, near, far, sample)
        message = silu(rows + edge).astype(BF)
        sums = dot(hot, message).astype(BF)
        out[sample] = sums
        out[sample + 2] = sums


def start_kernel(parts, gain, out):
    total = parts[0].astype(F32)
    for section in range(1, parts.shape[0]):
        total = total + parts[section].astype(F32)
    out[...] = layer_norm(total, gain[...]).astype(BF)


def outgoing(core, state, halo_hot, coarse_out, halo_out, inner_out):
    rows = dot(halo_hot[...], state).astype(BF)
    halo_out[...] = jnp.where(core[0] == 0, rows[3 * HALO : 6 * HALO], rows[: 3 * HALO])
    inner_out[...] = rows[6 * HALO :]
    pair = jnp.concatenate([state[0:1].astype(F32), state[ROWS : ROWS + 1].astype(F32)], axis=0)
    coarse_out[...] = jnp.broadcast_to(pair.astype(BF)[None], coarse_out.shape)


def prepare_kernel(core, state, halo_hot, coarse_out, halo_out, inner_out):
    outgoing(core, state[...], halo_hot, coarse_out, halo_out, inner_out)


def fetch_weights(core, wbuf, ebuf, sems, mine, other):
    size = wbuf.shape[1]

    def start(m):
        at = pl.ds((m % 2) * size, size)

        @pl.when(core[0] == m // 2)
        def _():
            pltpu.make_async_copy(mine.at[at], wbuf.at[m], sems.at[m]).start()

        @pl.when(core[0] != m // 2)
        def _():
            pltpu.make_async_copy(other.at[at], wbuf.at[m], sems.at[m]).start()

        return pltpu.make_async_copy(mine.at[at], wbuf.at[m], sems.at[m])

    tail = pltpu.make_async_copy(mine.at[pl.ds(2 * size, EXTRA)], ebuf, sems.at[4])
    return start, tail


def layer_kernel(core, *refs, layer, last):
    refs = list(refs)

    def take(count):
        taken = refs[:count]
        del refs[:count]
        return taken

    state, halo, inner, coarse, edges_hot, sums_hot, tail_from = take(7)
    mine, other = take(2)
    outs = take(1 if last else 4)
    wbuf, ebuf, sources, table, hot, sums, tail_weight, sems = take(8)
    staged = take(len(outs))
    (out_sems,) = refs

    at_halo = 2 * ROWS
    at_inner = at_halo + 6 * HALO
    at_coarse = at_inner + 2 * HALO
    coarse_rows = coarse.shape[0]
    in_place = [
        pltpu.make_async_copy(source, sources.at[pl.ds(at, count)], sems.at[5 + i])
        for i, (source, at, count) in enumerate(
            (
                (state, 0, 2 * ROWS),
                (halo.at[0, 0], at_halo, 3 * HALO),
                (halo.at[1, 1], at_halo + 3 * HALO, 3 * HALO),
                (inner, at_inner, 2 * HALO),
                (coarse, at_coarse, coarse_rows),
            )
        )
    ]
    for copy in in_place:
        copy.start()
    later = [
        pltpu.make_async_copy(edges_hot, hot, sems.at[10]),
        pltpu.make_async_copy(sums_hot, sums, sems.at[11]),
        pltpu.make_async_copy(tail_from.at[0] if last else tail_from, tail_weight, sems.at[12]),
    ]
    start, vectors = fetch_weights(core, wbuf, ebuf, sems, mine.at[layer], other.at[layer])
    waits = [start(0), start(1)]
    vectors.start()
    later[0].start()
    later[1].start()
    waits += [start(2), start(3), vectors]
    later[2].start()

    for copy in in_place:
        copy.wait()
    waits[0].wait()
    keys = dot(sources[...], wbuf[0]).astype(BF)
    waits[1].wait()
    old = sources[0:at_halo]
    target = dot(old, wbuf[1]).astype(BF)
    up, down = at_halo, at_halo + 3 * HALO
    halo_from = (
        (up + HALO, at_inner, up, down + HALO),
        (at_inner + HALO, down, up + 2 * HALO, down + 2 * HALO),
    )
    at_target = ROWS + 4 * HALO + coarse_rows
    waits[4].wait()
    later[0].wait()
    later[1].wait()
    nodes = []
    for owner in range(2):
        table[owner, 0:ROWS] = keys[owner * ROWS : (owner + 1) * ROWS]
        for block in range(4):
            source = halo_from[owner][block]
            table[owner, ROWS + block * HALO : ROWS + (block + 1) * HALO] = keys[source : source + HALO]
        table[owner, ROWS + 4 * HALO : at_target] = keys[at_coarse : at_coarse + coarse_rows]
        table[owner, at_target : at_target + ROWS] = target[owner * ROWS : (owner + 1) * ROWS]
        table[owner, at_target + ROWS :] = ebuf[...]
        hidden = silu(dot(hot[owner], table[owner])).astype(BF)
        nodes.append(dot(sums[owner], hidden).astype(BF))
    node_in = jnp.concatenate(nodes, axis=0)
    waits[3].wait()
    kept = dot(old, wbuf[3])
    waits[2].wait()

    def vector(at):
        return (ebuf[at : at + 1].astype(F32) + ebuf[at + 1 : at + 2].astype(F32)) + ebuf[
            at + 2 : at + 3
        ].astype(F32)

    update = silu(dot(node_in, wbuf[2]) + kept + vector(NODE_BIAS))
    new = (old.astype(F32) + layer_norm(update, vector(GAIN))).astype(BF)
    later[2].wait()
    if last:
        rows = jnp.where(core[0] == 0, new[:ROWS], new[ROWS:])
        projected = dot(rows, tail_weight[...]).astype(BF)
        staged[0][...] = projected
    else:
        staged[0][...] = new
        outgoing(core, new, tail_weight, *staged[1:])
    sent = [pltpu.make_async_copy(a, b, out_sems.at[i]) for i, (a, b) in enumerate(zip(staged, outs))]
    for copy in sent:
        copy.start()
    for copy in sent:
        copy.wait()


def deliver_kernel(core, keys, senders, own, near, far):
    both = jnp.concatenate([keys[0], keys[1]], axis=0)
    send_blocks(core, both, senders, own, near, far)


def decode_kernel(core, own, near, far, queries, features, weight, bias, receivers, x, out_weight, out):
    edge = edge_term(features[...], weight[...]) + bias[...]
    hot = hot_rows(receivers[...], ROWS)
    width = out_weight.shape[1]
    for sample in range(2):
        at = pl.ds(sample * ROWS, ROWS)
        rows = arrived_rows(core, own, near, far, sample)
        hidden = silu(rows + dot_t(hot, queries[at]) + edge).astype(BF)
        total = dot(hot, hidden).astype(BF)
        change = dot(total, out_weight[...])
        out[sample] = (x[at, :width].astype(F32) + change).astype(BF)


def shards(
    grid_inputs, embed_weight, embed_bias, encode_weight, encode_edge_weight, encode_bias, mesh_gain,
    process_weight, process_edge_weight, process_bias, process_gain, decode_weight, decode_edge_weight,
    decode_bias, output_weight, encode_senders, encode_receivers, encode_features, halo_send_rows,
    mesh_senders, mesh_receivers, mesh_features, decode_senders, decode_receivers, decode_features,
):
    samples, grid_rows, in_width = grid_inputs.shape
    latent = embed_weight.shape[1]
    owners = lax.axis_size("space")
    chips = owners // 2
    sections = lax.axis_size("section")
    section = lax.axis_index("section")
    core_id = lax.axis_index("space") % 2
    core = jnp.stack([core_id, section % 2]).astype(jnp.int32)
    pairs = [[2 * k, 2 * k + 1] for k in range(chips)]
    same_core = [[2 * k + c for k in range(chips)] for c in range(2)]
    crossings = [[2 * k + 1, (2 * k + 2) % owners] for k in range(chips)]
    swap = [(i, i ^ 1) for i in range(owners)]

    def gather_pair(value):
        return lax.all_gather(value, "space", axis=0, axis_index_groups=pairs)

    def gather_crossing(value):
        return lax.all_gather(value, "space", axis=0, axis_index_groups=crossings)

    def vec(value):
        return value.reshape(1, -1)

    half_rows = 2 * latent + EXTRA
    half = call(
        pack_weights_kernel,
        shape((half_rows, latent)),
        core, process_edge_weight[0], process_bias[0], process_gain, process_weight[0],
        smem=1, hbm=4, hbm_out=True,
        scratch=[
            pltpu.VMEM(process_edge_weight.shape[1:], F32),
            pltpu.VMEM(process_bias.shape[1:], F32),
            pltpu.VMEM(process_gain.shape, F32),
            pltpu.VMEM((half_rows, latent), BF),
            pltpu.SemaphoreType.DMA((5,)),
        ],
    )
    gathered = lax.all_gather(half, "section", axis=0)

    grid_inputs, half = lax.optimization_barrier((grid_inputs, half))
    x = grid_inputs.reshape(samples * grid_rows, in_width)
    cap = encode_senders.shape[2] // 3
    block = shape((samples * cap, latent))
    own, near, far, queries = call(
        embed_kernel,
        (block, block, block, shape((samples * grid_rows, latent))),
        core, x, embed_weight, vec(embed_bias), encode_weight, decode_weight, encode_senders[0],
        smem=1,
    )
    far = gather_crossing(far)
    near = gather_pair(near)
    edges = mesh_senders.shape[1]
    b = halo_send_rows.reshape(4, HALO)
    none = jnp.zeros((HALO,), jnp.int32)
    low = jnp.concatenate([b[2], none, none, b[1], b[3], none, none, b[0]])
    high = jnp.concatenate([none, b[0] + ROWS, b[2] + ROWS, none, none, b[3] + ROWS, b[1] + ROWS, none])
    halo_list = jnp.pad(jnp.where(core_id == 0, low, high), (0, edges - 8 * HALO))
    meta = jnp.concatenate(
        [
            jnp.stack([mesh_senders[0], mesh_receivers[0], halo_list, jnp.zeros_like(halo_list)]).astype(F32),
            mesh_features[:, 0, :],
        ],
        axis=0,
    )
    meta = gather_pair(meta)
    table_rows = 2 * ROWS + 4 * HALO + owners + EXTRA
    edges_hot, sums_hot, halo_hot = call(
        functools.partial(setup_kernel, coarse=owners),
        (shape((2, edges, table_rows)), shape((2, ROWS, edges)), shape((8 * HALO, 2 * ROWS))),
        meta,
    )
    parts = call(
        message_kernel,
        shape((sections, ROWS, latent)),
        core, own, near, far, encode_features[:, 0, 0, :], encode_edge_weight, vec(encode_bias), encode_receivers[0],
        smem=1,
    )
    parts = lax.all_to_all(parts, "section", 0, 0, tiled=True)
    start = call(start_kernel, shape((ROWS, latent)), parts, vec(mesh_gain))
    state = gather_pair(start).reshape(2 * ROWS, latent)

    outgoing_shapes = (
        shape((chips, 2, latent)),
        shape((3 * HALO, latent)),
        shape((2 * HALO, latent)),
    )
    scratch = [
        pltpu.VMEM((4, latent, latent), BF),
        pltpu.VMEM((EXTRA, latent), BF),
        pltpu.VMEM((2 * ROWS + 8 * HALO + owners, latent), BF),
        pltpu.VMEM((2, table_rows, latent), BF),
        pltpu.VMEM((2, edges, table_rows), BF),
        pltpu.VMEM((2, ROWS, edges), BF),
    ]
    coarse, halo, inner = call(prepare_kernel, outgoing_shapes, core, state, halo_hot, smem=1)
    for layer in range(4):
        coarse = lax.all_to_all(coarse, "space", 0, 0, tiled=True, axis_index_groups=same_core)
        coarse = coarse.reshape(owners, latent)
        halo = gather_pair(gather_crossing(halo))
        if layer == 0:
            gathered, coarse = lax.optimization_barrier((gathered, coarse))
            gathered_other = lax.ppermute(gathered, "space", swap)
        last = layer == 3
        tail = decode_weight if last else halo_hot
        weights = (gathered, gathered_other)
        inputs = (state, halo, inner, coarse, edges_hot, sums_hot, tail) + weights
        out = (shape((ROWS, latent)),) if last else (shape(state.shape),) + outgoing_shapes
        out = call(
            functools.partial(layer_kernel, layer=layer, last=last),
            out, core, *inputs,
            smem=1, hbm=len(inputs), hbm_out=True, limit=LAYER_LIMIT,
            scratch=scratch
            + [pltpu.VMEM(tail.shape[-2:], BF), pltpu.SemaphoreType.DMA((13,))]
            + [pltpu.VMEM(o.shape, BF) for o in out]
            + [pltpu.SemaphoreType.DMA((4,))],
        )
        if last:
            keys = out[0]
        else:
            state, coarse, halo, inner = out

    twins = [[i, i + 1] for i in range(0, sections, 2)]
    keys = lax.all_gather(keys, "section", axis=0, axis_index_groups=twins)
    own, near, far = call(deliver_kernel, (block, block, block), core, keys, decode_senders[0], smem=1)
    far = gather_crossing(far)
    near = gather_pair(near)
    return call(
        decode_kernel,
        shape((samples, grid_rows, output_weight.shape[1])),
        core, own, near, far, queries, decode_features[:, 0, 0, :], decode_edge_weight, vec(decode_bias),
        decode_receivers[0], x, output_weight,
        smem=1,
    )


def solution(mesh):
    return jax.shard_map(
        shards,
        mesh=mesh,
        in_specs=(
            P(None, ("section", "space"), None),
            P(),
            P(),
            P(),
            P(),
            P(),
            P(),
            P("section", None, None, None),
            P("section", None, None),
            P("section", None, None),
            P("section", None),
            P(),
            P(),
            P(),
            P(),
            P("section", "space", None),
            P("section", "space", None),
            P(None, "section", "space", None),
            P("space", None),
            P("space", None),
            P("space", None),
            P(None, "space", None),
            P("section", "space", None),
            P("section", "space", None),
            P(None, "section", "space", None),
        ),
        out_specs=P(None, ("section", "space"), None),
        check_vma=False,
    )
```

```python
import functools

import jax
import jax.numpy as jnp
from jax import lax
from jax.experimental import pallas as pl
from jax.experimental.pallas import tpu as pltpu
from jax.sharding import PartitionSpec as P

BF = jnp.bfloat16
F32 = jnp.float32
ROWS = 128
HALO = 16
EXTRA = 64
NODE_BIAS, GAIN = 32, 35
SMALL_LIMIT = 16 * 1024 * 1024
LAYER_LIMIT = 54000000
PACK_LIMIT = 64_900_000


def silu(v):
    return v * (0.5 + 0.5 * jnp.tanh(0.5 * v))


def dot(a, b):
    return jnp.dot(a, b, preferred_element_type=F32)


def dot_t(a, b):
    return lax.dot_general(a, b, (((0,), (0,)), ((), ())), preferred_element_type=F32)


def split3(x):
    hi = x.astype(BF)
    rest = x - hi.astype(F32)
    mid = rest.astype(BF)
    low = (rest - mid.astype(F32)).astype(BF)
    return hi, mid, low


def layer_norm(values, gain):
    center = values - jnp.mean(values, axis=-1, keepdims=True)
    spread = jnp.mean(center * center, axis=-1, keepdims=True)
    return center * lax.rsqrt(spread + 1e-05) * gain


def hot_rows(index_row, count):
    n = index_row.shape[1]
    return (lax.broadcasted_iota(jnp.int32, (count, n), 0) == index_row).astype(F32).astype(BF)


def feature_parts(features):
    hi, mid, low = split3(features)
    return jnp.concatenate([p.astype(F32) for p in (hi, hi, mid, mid, hi, low)], axis=0)


def weight_parts(weight):
    hi, mid, low = split3(weight)
    return jnp.concatenate([p.astype(F32) for p in (hi, mid, hi, mid, low, hi)], axis=0)


def edge_term(features, weight):
    return dot_t(feature_parts(features).astype(BF), weight_parts(weight).astype(BF))


def core_index():
    return lax.axis_index("space") % 2


def call(kernel, out, *args, hbm=0, scratch=(), hbm_out=False, limit=SMALL_LIMIT):
    count = len(args)
    specs = []
    for position in range(count):
        if position >= count - hbm:
            specs.append(pl.BlockSpec(memory_space=pltpu.HBM))
        else:
            specs.append(pl.BlockSpec(memory_space=pltpu.VMEM))
    out_spec = pl.BlockSpec(memory_space=pltpu.HBM if hbm_out else pltpu.VMEM)
    return pl.pallas_call(
        kernel,
        out_shape=out,
        in_specs=specs,
        out_specs=jax.tree.map(lambda _: out_spec, out),
        scratch_shapes=list(scratch),
        compiler_params=pltpu.CompilerParams(vmem_limit_bytes=limit),
        cost_estimate=pl.CostEstimate(flops=1_000_000, bytes_accessed=1_000_000, transcendentals=0),
    )(*args)


def shape(dims, dtype=BF):
    return jax.ShapeDtypeStruct(dims, dtype)


def pack_weights_kernel(edge_from, bias_from, gain_from, weight, out, edge_weight, bias, gain, packed, sems):
    size = weight.shape[1]
    half = 2 * size
    vectors = [
        pltpu.make_async_copy(source, target, sems.at[i])
        for i, (source, target) in enumerate(
            ((edge_from, edge_weight), (bias_from, bias), (gain_from, gain))
        )
    ]
    pieces = 4
    piece = half // pieces
    first = 2 * core_index()
    places = [pl.ds(i * piece, piece) for i in range(pieces)]
    matrices = [
        pltpu.make_async_copy(
            weight.at[first + i * piece // size, pl.ds(i * piece % size, piece)],
            packed.at[places[i]],
            sems.at[3 + i],
        )
        for i in range(pieces)
    ]
    packs = [
        pltpu.make_async_copy(packed.at[place], out.at[place], sems.at[3 + pieces + i])
        for i, place in enumerate(places + [pl.ds(half, EXTRA)])
    ]
    for copy in vectors + matrices:
        copy.start()
    for arrival, copy in zip(matrices, packs):
        arrival.wait()
        copy.start()
    for copy in vectors:
        copy.wait()
    width = edge_weight.shape[1]
    b_parts = [p.astype(F32) for p in split3(bias[0:1, :])]
    n_parts = [p.astype(F32) for p in split3(bias[1:2, :])]
    g_parts = [p.astype(F32) for p in split3(gain[...])]
    rows = jnp.concatenate(
        [weight_parts(edge_weight[...])]
        + b_parts
        + [jnp.zeros((5, width), F32)]
        + n_parts
        + g_parts
        + [jnp.zeros((EXTRA - 38, width), F32)],
        axis=0,
    )
    packed[half:] = rows.astype(BF)
    packs[pieces].start()
    for copy in packs:
        copy.wait()


def setup_kernel(meta, edges_out, sums_out, halo_out, *, coarse):
    edges = sums_out.shape[2]
    padded = -(-edges // 128) * 128
    table = edges_out.shape[2]
    target_at = ROWS + 4 * HALO + coarse
    extra_at = target_at + ROWS
    for owner in range(2):
        senders = meta[owner, 0:1, :].astype(jnp.int32)
        receivers = meta[owner, 1:2, :].astype(jnp.int32)
        pad = padded - edges
        features = meta[owner, 4:8, :]
        if pad:
            senders = jnp.concatenate([senders, jnp.full((1, pad), -1, jnp.int32)], axis=1)
            receivers_wide = jnp.concatenate([receivers, jnp.full((1, pad), -1000, jnp.int32)], axis=1)
            features = jnp.concatenate([features, jnp.zeros((4, pad), F32)], axis=1)
        else:
            receivers_wide = receivers
        row = lax.broadcasted_iota(jnp.int32, (extra_at, padded), 0)
        hot = ((row == senders) | (row == receivers_wide + target_at)).astype(F32)
        tail = jnp.concatenate(
            [
                feature_parts(features),
                jnp.ones((3, padded), F32),
                jnp.zeros((EXTRA - 27, padded), F32),
            ],
            axis=0,
        )
        whole = jnp.concatenate([hot, tail], axis=0)
        edges_out[owner] = jnp.transpose(whole)[:edges].astype(BF)
        sums_out[owner] = hot_rows(receivers, ROWS)
    sent = (meta[0, 2:3, 0 : 8 * HALO] + meta[1, 2:3, 0 : 8 * HALO]).astype(jnp.int32)
    hot = (lax.broadcasted_iota(jnp.int32, (2 * ROWS, 8 * HALO), 0) == sent).astype(F32)
    halo_out[...] = jnp.transpose(hot).astype(BF)


def embed_kernel(x, embed_weight, embed_bias, encode_weight, query_weight, senders, own, near, far, queries):
    latent = silu(dot(x[...], embed_weight[...]) + embed_bias[...]).astype(BF)
    keys = dot(latent, encode_weight[...]).astype(BF)
    send_blocks(keys, senders, own, near, far)
    queries[...] = dot(latent, query_weight[1]).astype(BF)


def send_blocks(keys, senders, own, near, far):
    first = core_index() == 0
    cap = senders.shape[1] // 3
    hot = hot_rows(senders[...], ROWS)
    for sample in range(2):
        rows = dot_t(hot, keys[sample * ROWS : (sample + 1) * ROWS]).astype(BF)
        out = pl.ds(sample * cap, cap)
        own[out] = rows[:cap]
        near[out] = jnp.where(first, rows[cap : 2 * cap], rows[2 * cap :])
        far[out] = jnp.where(first, rows[2 * cap :], rows[cap : 2 * cap])


def arrived_rows(own, near, far, sample):
    first = core_index() == 0
    cap = own.shape[0] // 2
    at = pl.ds(sample * cap, cap)
    from_near = jnp.where(first, near[1, at], near[0, at])
    from_far = jnp.where(first, far[0, at], far[1, at])
    return jnp.concatenate(
        [own[at], jnp.where(first, from_far, from_near), jnp.where(first, from_near, from_far)],
        axis=0,
    ).astype(F32)


def message_kernel(own, near, far, features, weight, bias, receivers, out):
    edge = edge_term(features[...], weight[...]) + bias[...]
    hot = hot_rows(receivers[...], ROWS)
    for sample in range(2):
        rows = arrived_rows(own, near, far, sample)
        message = silu(rows + edge).astype(BF)
        sums = dot(hot, message).astype(BF)
        out[sample] = sums
        out[sample + 2] = sums


def start_kernel(parts, gain, out):
    total = parts[0].astype(F32)
    for section in range(1, parts.shape[0]):
        total = total + parts[section].astype(F32)
    out[...] = layer_norm(total, gain[...]).astype(BF)


def outgoing(state, halo_hot, coarse_out, halo_out, inner_out):
    rows = dot(halo_hot[...], state).astype(BF)
    halo_out[...] = jnp.where(core_index() == 0, rows[3 * HALO : 6 * HALO], rows[: 3 * HALO])
    inner_out[...] = rows[6 * HALO :]
    pair = jnp.concatenate([state[0:1].astype(F32), state[ROWS : ROWS + 1].astype(F32)], axis=0)
    coarse_out[...] = jnp.broadcast_to(pair.astype(BF)[None], coarse_out.shape)


def prepare_kernel(state, halo_hot, coarse_out, halo_out, inner_out):
    outgoing(state[...], halo_hot, coarse_out, halo_out, inner_out)


def fetch(m, target, sem, mine, other):
    size = target.shape[0]
    at = pl.ds((m % 2) * size, size)

    @pl.when(core_index() == m // 2)
    def _():
        pltpu.make_async_copy(mine.at[at], target, sem).start()

    @pl.when(core_index() != m // 2)
    def _():
        pltpu.make_async_copy(other.at[at], target, sem).start()

    return pltpu.make_async_copy(mine.at[at], target, sem)


def layer_kernel(*refs, layer, last):
    refs = list(refs)

    def take(count):
        taken = refs[:count]
        del refs[:count]
        return taken

    state, halo, inner, coarse, hot, sums, tail_weight = take(7)
    mine, other = take(2)
    outs = take(1 if last else 4)
    wbuf, ebuf, sources, table, sems = refs
    size = wbuf.shape[1]
    here = mine.at[layer]
    there = other if layer == 0 else other.at[layer]
    first = [fetch(m, wbuf.at[m], sems.at[m], here, there) for m in range(2)]
    vectors = pltpu.make_async_copy(here.at[pl.ds(2 * size, EXTRA)], ebuf, sems.at[4])
    vectors.start()
    second = [fetch(m, wbuf.at[m], sems.at[m], here, there) for m in (3, 2)]
    at_halo = 2 * ROWS
    at_inner = at_halo + 6 * HALO
    at_coarse = at_inner + 2 * HALO
    coarse_rows = coarse.shape[0]
    sources[0:at_halo] = state[...]
    sources[at_halo : at_halo + 3 * HALO] = halo[0, 0]
    sources[at_halo + 3 * HALO : at_inner] = halo[1, 1]
    sources[at_inner:at_coarse] = inner[...]
    sources[at_coarse:] = coarse[...]
    first[0].wait()
    keys = dot(sources[...], wbuf[0]).astype(BF)
    first[1].wait()
    old = state[...]
    target = dot(old, wbuf[1]).astype(BF)
    up, down = at_halo, at_halo + 3 * HALO
    halo_from = (
        (up + HALO, at_inner, up, down + HALO),
        (at_inner + HALO, down, up + 2 * HALO, down + 2 * HALO),
    )
    at_target = ROWS + 4 * HALO + coarse_rows
    vectors.wait()
    nodes = []
    for owner in range(2):
        table[owner, 0:ROWS] = keys[owner * ROWS : (owner + 1) * ROWS]
        for block in range(4):
            source = halo_from[owner][block]
            table[owner, ROWS + block * HALO : ROWS + (block + 1) * HALO] = keys[source : source + HALO]
        table[owner, ROWS + 4 * HALO : at_target] = keys[at_coarse : at_coarse + coarse_rows]
        table[owner, at_target : at_target + ROWS] = target[owner * ROWS : (owner + 1) * ROWS]
        table[owner, at_target + ROWS :] = ebuf[...]
        hidden = silu(dot(hot[owner], table[owner])).astype(BF)
        nodes.append(dot(sums[owner], hidden).astype(BF))
    node_in = jnp.concatenate(nodes, axis=0)
    second[0].wait()
    kept = dot(old, wbuf[3])
    second[1].wait()

    def vector(at):
        return (ebuf[at : at + 1].astype(F32) + ebuf[at + 1 : at + 2].astype(F32)) + ebuf[
            at + 2 : at + 3
        ].astype(F32)

    update = silu(dot(node_in, wbuf[2]) + kept + vector(NODE_BIAS))
    new = (old.astype(F32) + layer_norm(update, vector(GAIN))).astype(BF)
    if last:
        rows = jnp.where(core_index() == 0, new[:ROWS], new[ROWS:])
        outs[0][...] = dot(rows, tail_weight[0]).astype(BF)
    else:
        outs[0][...] = new
        outgoing(new, tail_weight, *outs[1:])


def deliver_kernel(keys, senders, own, near, far):
    both = jnp.concatenate([keys[0], keys[1]], axis=0)
    send_blocks(both, senders, own, near, far)


def decode_kernel(own, near, far, queries, features, weight, bias, receivers, x, out_weight, out):
    edge = edge_term(features[...], weight[...]) + bias[...]
    hot = hot_rows(receivers[...], ROWS)
    width = out_weight.shape[1]
    for sample in range(2):
        at = pl.ds(sample * ROWS, ROWS)
        rows = arrived_rows(own, near, far, sample)
        hidden = silu(rows + dot_t(hot, queries[at]) + edge).astype(BF)
        total = dot(hot, hidden).astype(BF)
        change = dot(total, out_weight[...])
        out[sample] = (x[at, :width].astype(F32) + change).astype(BF)


def shards(
    grid_inputs, embed_weight, embed_bias, encode_weight, encode_edge_weight, encode_bias, mesh_gain,
    process_weight, process_edge_weight, process_bias, process_gain, decode_weight, decode_edge_weight,
    decode_bias, output_weight, encode_senders, encode_receivers, encode_features, halo_send_rows,
    mesh_senders, mesh_receivers, mesh_features, decode_senders, decode_receivers, decode_features,
):
    samples, grid_rows, in_width = grid_inputs.shape
    latent = embed_weight.shape[1]
    owners = lax.axis_size("space")
    chips = owners // 2
    sections = lax.axis_size("section")
    core_id = lax.axis_index("space") % 2
    pairs = [[2 * k, 2 * k + 1] for k in range(chips)]
    same_core = [[2 * k + c for k in range(chips)] for c in range(2)]
    crossings = [[2 * k + 1, (2 * k + 2) % owners] for k in range(chips)]
    swap = [(i, i ^ 1) for i in range(owners)]

    def gather_pair(value):
        return lax.all_gather(value, "space", axis=0, axis_index_groups=pairs)

    def gather_crossing(value):
        return lax.all_gather(value, "space", axis=0, axis_index_groups=crossings)

    def vec(value):
        return value.reshape(1, -1)

    half_rows = 2 * latent + EXTRA
    half = call(
        pack_weights_kernel,
        shape((half_rows, latent)),
        process_edge_weight[0], process_bias[0], process_gain, process_weight[0],
        hbm=4, hbm_out=True, limit=PACK_LIMIT,
        scratch=[
            pltpu.VMEM(process_edge_weight.shape[1:], F32),
            pltpu.VMEM(process_bias.shape[1:], F32),
            pltpu.VMEM(process_gain.shape, F32),
            pltpu.VMEM((half_rows, latent), BF),
            pltpu.SemaphoreType.DMA((12,)),
        ],
    )
    gathered = lax.all_gather(half, "section", axis=0)

    grid_inputs, half = lax.optimization_barrier((grid_inputs, half))
    x = grid_inputs.reshape(samples * grid_rows, in_width)
    cap = encode_senders.shape[2] // 3
    block = shape((samples * cap, latent))
    own, near, far, queries = call(
        embed_kernel,
        (block, block, block, shape((samples * grid_rows, latent))),
        x, embed_weight, vec(embed_bias), encode_weight, decode_weight, encode_senders[0],
    )
    far = gather_crossing(far)
    near = gather_pair(near)
    edges = mesh_senders.shape[1]
    b = halo_send_rows.reshape(4, HALO)
    none = jnp.zeros((HALO,), jnp.int32)
    low = jnp.concatenate([b[2], none, none, b[1], b[3], none, none, b[0]])
    high = jnp.concatenate([none, b[0] + ROWS, b[2] + ROWS, none, none, b[3] + ROWS, b[1] + ROWS, none])
    halo_list = jnp.pad(jnp.where(core_id == 0, low, high), (0, edges - 8 * HALO))
    meta = jnp.concatenate(
        [
            jnp.stack([mesh_senders[0], mesh_receivers[0], halo_list, jnp.zeros_like(halo_list)]).astype(F32),
            mesh_features[:, 0, :],
        ],
        axis=0,
    )
    meta = gather_pair(meta)
    table_rows = 2 * ROWS + 4 * HALO + owners + EXTRA
    edges_hot, sums_hot, halo_hot = call(
        functools.partial(setup_kernel, coarse=owners),
        (shape((2, edges, table_rows)), shape((2, ROWS, edges)), shape((8 * HALO, 2 * ROWS))),
        meta,
    )
    parts = call(
        message_kernel,
        shape((sections, ROWS, latent)),
        own, near, far, encode_features[:, 0, 0, :], encode_edge_weight, vec(encode_bias), encode_receivers[0],
    )
    parts = lax.all_to_all(parts, "section", 0, 0, tiled=True)
    start = call(start_kernel, shape((ROWS, latent)), parts, vec(mesh_gain))
    state = gather_pair(start).reshape(2 * ROWS, latent)

    outgoing_shapes = (
        shape((chips, 2, latent)),
        shape((3 * HALO, latent)),
        shape((2 * HALO, latent)),
    )
    scratch = [
        pltpu.VMEM((4, latent, latent), BF),
        pltpu.VMEM((EXTRA, latent), BF),
        pltpu.VMEM((2 * ROWS + 8 * HALO + owners, latent), BF),
        pltpu.VMEM((2, table_rows, latent), BF),
        pltpu.SemaphoreType.DMA((5,)),
    ]
    coarse, halo, inner = call(prepare_kernel, outgoing_shapes, state, halo_hot)
    for layer in range(4):
        coarse = lax.all_to_all(coarse, "space", 0, 0, tiled=True, axis_index_groups=same_core)
        coarse = coarse.reshape(owners, latent)
        halo = gather_pair(gather_crossing(halo))
        if layer == 0:
            gathered, halo, coarse = lax.optimization_barrier((gathered, halo, coarse))
            gathered_other = lax.ppermute(gathered[0], "space", swap)
        last = layer == 3
        tail = decode_weight if last else halo_hot
        weights = (gathered, gathered_other)
        inputs = (state, halo, inner, coarse, edges_hot, sums_hot, tail) + weights
        if last:
            out = (shape((ROWS, latent)),)
        else:
            out = (shape(state.shape),) + outgoing_shapes
        out = call(
            functools.partial(layer_kernel, layer=layer, last=last),
            out, *inputs,
            hbm=2, limit=LAYER_LIMIT, scratch=scratch,
        )
        if last:
            keys = out[0]
        else:
            state, coarse, halo, inner = out
        if layer == 0:
            gathered, state = lax.optimization_barrier((gathered, state))
            gathered_other = lax.ppermute(gathered, "space", swap)

    twins = [[i, i + 1] for i in range(0, sections, 2)]
    keys = lax.all_gather(keys, "section", axis=0, axis_index_groups=twins)
    own, near, far = call(deliver_kernel, (block, block, block), keys, decode_senders[0])
    far = gather_crossing(far)
    near = gather_pair(near)
    return call(
        decode_kernel,
        shape((samples, grid_rows, output_weight.shape[1])),
        own, near, far, queries, decode_features[:, 0, 0, :], decode_edge_weight, vec(decode_bias),
        decode_receivers[0], x, output_weight,
    )


def solution(mesh):
    return jax.shard_map(
        shards,
        mesh=mesh,
        in_specs=(
            P(None, ("section", "space"), None),
            P(),
            P(),
            P(),
            P(),
            P(),
            P(),
            P("section", None, None, None),
            P("section", None, None),
            P("section", None, None),
            P("section", None),
            P(),
            P(),
            P(),
            P(),
            P("section", "space", None),
            P("section", "space", None),
            P(None, "section", "space", None),
            P("space", None),
            P("space", None),
            P("space", None),
            P(None, "space", None),
            P("section", "space", None),
            P("section", "space", None),
            P(None, "section", "space", None),
        ),
        out_specs=P(None, ("section", "space"), None),
        check_vma=False,
    )
```

```python
import functools

import jax
import jax.numpy as jnp
from jax import lax
from jax.experimental import pallas as pl
from jax.experimental.pallas import tpu as pltpu
from jax.sharding import PartitionSpec as P

BF = jnp.bfloat16
F32 = jnp.float32
ROWS = 128
HALO = 16
EXTRA = 64
NODE_BIAS, GAIN = 32, 35
SMALL_LIMIT = 16 * 1024 * 1024
FIRST_LIMIT = 51000000
LAYER_LIMIT = 54000000
PACK_LIMIT = 64_900_000


def silu(v):
    return v * (0.5 + 0.5 * jnp.tanh(0.5 * v))


def dot(a, b):
    return jnp.dot(a, b, preferred_element_type=F32)


def dot_t(a, b):
    return lax.dot_general(a, b, (((0,), (0,)), ((), ())), preferred_element_type=F32)


def split3(x):
    hi = x.astype(BF)
    rest = x - hi.astype(F32)
    mid = rest.astype(BF)
    low = (rest - mid.astype(F32)).astype(BF)
    return hi, mid, low


def layer_norm(values, gain):
    center = values - jnp.mean(values, axis=-1, keepdims=True)
    spread = jnp.mean(center * center, axis=-1, keepdims=True)
    return center * lax.rsqrt(spread + 1e-05) * gain


def hot_rows(index_row, count):
    n = index_row.shape[1]
    return (lax.broadcasted_iota(jnp.int32, (count, n), 0) == index_row).astype(F32).astype(BF)


def feature_parts(features):
    hi, mid, low = split3(features)
    return jnp.concatenate([p.astype(F32) for p in (hi, hi, mid, mid, hi, low)], axis=0)


def weight_parts(weight):
    hi, mid, low = split3(weight)
    return jnp.concatenate([p.astype(F32) for p in (hi, mid, hi, mid, low, hi)], axis=0)


def edge_term(features, weight):
    return dot_t(feature_parts(features).astype(BF), weight_parts(weight).astype(BF))


def core_index():
    return lax.axis_index("space") % 2


def call(kernel, out, *args, hbm=0, scratch=(), hbm_out=False, limit=SMALL_LIMIT):
    count = len(args)
    specs = []
    for position in range(count):
        if position >= count - hbm:
            specs.append(pl.BlockSpec(memory_space=pltpu.HBM))
        else:
            specs.append(pl.BlockSpec(memory_space=pltpu.VMEM))
    out_spec = pl.BlockSpec(memory_space=pltpu.HBM if hbm_out else pltpu.VMEM)
    return pl.pallas_call(
        kernel,
        out_shape=out,
        in_specs=specs,
        out_specs=jax.tree.map(lambda _: out_spec, out),
        scratch_shapes=list(scratch),
        compiler_params=pltpu.CompilerParams(vmem_limit_bytes=limit),
        cost_estimate=pl.CostEstimate(flops=1_000_000, bytes_accessed=1_000_000, transcendentals=0),
    )(*args)


def shape(dims, dtype=BF):
    return jax.ShapeDtypeStruct(dims, dtype)


def pack_weights_kernel(edge_from, bias_from, gain_from, weight, out, edge_weight, bias, gain, packed, sems):
    size = weight.shape[1]
    half = 2 * size
    vectors = [
        pltpu.make_async_copy(source, target, sems.at[i])
        for i, (source, target) in enumerate(
            ((edge_from, edge_weight), (bias_from, bias), (gain_from, gain))
        )
    ]
    pieces = 4
    piece = half // pieces
    first = 2 * core_index()
    places = [pl.ds(i * piece, piece) for i in range(pieces)]
    matrices = [
        pltpu.make_async_copy(
            weight.at[first + i * piece // size, pl.ds(i * piece % size, piece)],
            packed.at[places[i]],
            sems.at[3 + i],
        )
        for i in range(pieces)
    ]
    packs = [
        pltpu.make_async_copy(packed.at[place], out.at[place], sems.at[3 + pieces + i])
        for i, place in enumerate(places + [pl.ds(half, EXTRA)])
    ]
    for copy in vectors + matrices:
        copy.start()
    for arrival, copy in zip(matrices, packs):
        arrival.wait()
        copy.start()
    for copy in vectors:
        copy.wait()
    width = edge_weight.shape[1]
    b_parts = [p.astype(F32) for p in split3(bias[0:1, :])]
    n_parts = [p.astype(F32) for p in split3(bias[1:2, :])]
    g_parts = [p.astype(F32) for p in split3(gain[...])]
    rows = jnp.concatenate(
        [weight_parts(edge_weight[...])]
        + b_parts
        + [jnp.zeros((5, width), F32)]
        + n_parts
        + g_parts
        + [jnp.zeros((EXTRA - 38, width), F32)],
        axis=0,
    )
    packed[half:] = rows.astype(BF)
    packs[pieces].start()
    for copy in packs:
        copy.wait()


def setup_kernel(meta, edges_out, sums_out, halo_out, *, coarse):
    edges = sums_out.shape[2]
    padded = -(-edges // 128) * 128
    table = edges_out.shape[2]
    target_at = ROWS + 4 * HALO + coarse
    extra_at = target_at + ROWS
    for owner in range(2):
        senders = meta[owner, 0:1, :].astype(jnp.int32)
        receivers = meta[owner, 1:2, :].astype(jnp.int32)
        pad = padded - edges
        features = meta[owner, 4:8, :]
        if pad:
            senders = jnp.concatenate([senders, jnp.full((1, pad), -1, jnp.int32)], axis=1)
            receivers_wide = jnp.concatenate([receivers, jnp.full((1, pad), -1000, jnp.int32)], axis=1)
            features = jnp.concatenate([features, jnp.zeros((4, pad), F32)], axis=1)
        else:
            receivers_wide = receivers
        row = lax.broadcasted_iota(jnp.int32, (extra_at, padded), 0)
        hot = ((row == senders) | (row == receivers_wide + target_at)).astype(F32)
        tail = jnp.concatenate(
            [
                feature_parts(features),
                jnp.ones((3, padded), F32),
                jnp.zeros((EXTRA - 27, padded), F32),
            ],
            axis=0,
        )
        whole = jnp.concatenate([hot, tail], axis=0)
        edges_out[owner] = jnp.transpose(whole)[:edges].astype(BF)
        sums_out[owner] = hot_rows(receivers, ROWS)
    sent = (meta[0, 2:3, 0 : 8 * HALO] + meta[1, 2:3, 0 : 8 * HALO]).astype(jnp.int32)
    hot = (lax.broadcasted_iota(jnp.int32, (2 * ROWS, 8 * HALO), 0) == sent).astype(F32)
    halo_out[...] = jnp.transpose(hot).astype(BF)


def embed_kernel(x, embed_weight, embed_bias, encode_weight, query_weight, senders, own, near, far, queries):
    latent = silu(dot(x[...], embed_weight[...]) + embed_bias[...]).astype(BF)
    keys = dot(latent, encode_weight[...]).astype(BF)
    send_blocks(keys, senders, own, near, far)
    queries[...] = dot(latent, query_weight[1]).astype(BF)


def send_blocks(keys, senders, own, near, far):
    first = core_index() == 0
    cap = senders.shape[1] // 3
    hot = hot_rows(senders[...], ROWS)
    for sample in range(2):
        rows = dot_t(hot, keys[sample * ROWS : (sample + 1) * ROWS]).astype(BF)
        out = pl.ds(sample * cap, cap)
        own[out] = rows[:cap]
        near[out] = jnp.where(first, rows[cap : 2 * cap], rows[2 * cap :])
        far[out] = jnp.where(first, rows[2 * cap :], rows[cap : 2 * cap])


def arrived_rows(own, near, far, sample):
    first = core_index() == 0
    cap = own.shape[0] // 2
    at = pl.ds(sample * cap, cap)
    from_near = jnp.where(first, near[1, at], near[0, at])
    from_far = jnp.where(first, far[0, at], far[1, at])
    return jnp.concatenate(
        [own[at], jnp.where(first, from_far, from_near), jnp.where(first, from_near, from_far)],
        axis=0,
    ).astype(F32)


def feature_rows(features):
    return jnp.concatenate([features[c] for c in range(features.shape[0])], axis=0)


def message_kernel(own, near, far, features, weight, bias, receivers, out):
    edge = edge_term(feature_rows(features), weight[...]) + bias[...]
    hot = hot_rows(receivers[...], ROWS)
    for sample in range(2):
        rows = arrived_rows(own, near, far, sample)
        message = silu(rows + edge).astype(BF)
        sums = dot(hot, message).astype(BF)
        out[sample] = sums
        out[sample + 2] = sums


def start_kernel(parts, gain, out):
    total = parts[0].astype(F32)
    for section in range(1, parts.shape[0]):
        total = total + parts[section].astype(F32)
    out[...] = layer_norm(total, gain[...]).astype(BF)


def outgoing(state, halo_hot, coarse_out, halo_out, inner_out):
    rows = dot(halo_hot[...], state).astype(BF)
    halo_out[...] = jnp.where(core_index() == 0, rows[3 * HALO : 6 * HALO], rows[: 3 * HALO])
    inner_out[...] = rows[6 * HALO :]
    pair = jnp.concatenate([state[0:1].astype(F32), state[ROWS : ROWS + 1].astype(F32)], axis=0)
    coarse_out[...] = jnp.broadcast_to(pair.astype(BF)[None], coarse_out.shape)


def prepare_kernel(state, halo_hot, coarse_out, halo_out, inner_out):
    outgoing(state[...], halo_hot, coarse_out, halo_out, inner_out)


def fetch(m, target, sem, mine, other):
    size = target.shape[0]
    at = pl.ds((m % 2) * size, size)

    @pl.when(core_index() == m // 2)
    def _():
        pltpu.make_async_copy(mine.at[at], target, sem).start()

    @pl.when(core_index() != m // 2)
    def _():
        pltpu.make_async_copy(other.at[at], target, sem).start()

    return pltpu.make_async_copy(mine.at[at], target, sem)


def layer_kernel(*refs, layer, last):
    refs = list(refs)

    def take(count):
        taken = refs[:count]
        del refs[:count]
        return taken

    state, halo, inner, coarse, hot, sums, tail_weight = take(7)
    mine, other = take(2)
    outs = take(1 if last else 4)
    wbuf, ebuf, sources, table, sems = refs
    size = wbuf.shape[1]
    here = mine.at[layer]
    there = other if layer == 0 else other.at[layer]
    first = [fetch(m, wbuf.at[m], sems.at[m], here, there) for m in range(2)]
    vectors = pltpu.make_async_copy(here.at[pl.ds(2 * size, EXTRA)], ebuf, sems.at[4])
    vectors.start()
    second = [fetch(m, wbuf.at[m], sems.at[m], here, there) for m in (3, 2)]
    at_halo = 2 * ROWS
    at_inner = at_halo + 6 * HALO
    at_coarse = at_inner + 2 * HALO
    coarse_rows = coarse.shape[0]
    sources[0:at_halo] = state[...]
    sources[at_halo : at_halo + 3 * HALO] = halo[0, 0]
    sources[at_halo + 3 * HALO : at_inner] = halo[1, 1]
    sources[at_inner:at_coarse] = inner[...]
    sources[at_coarse:] = coarse[...]
    first[0].wait()
    keys = dot(sources[...], wbuf[0]).astype(BF)
    first[1].wait()
    old = state[...]
    target = dot(old, wbuf[1]).astype(BF)
    up, down = at_halo, at_halo + 3 * HALO
    halo_from = (
        (up + HALO, at_inner, up, down + HALO),
        (at_inner + HALO, down, up + 2 * HALO, down + 2 * HALO),
    )
    at_target = ROWS + 4 * HALO + coarse_rows
    vectors.wait()
    nodes = []
    for owner in range(2):
        table[owner, 0:ROWS] = keys[owner * ROWS : (owner + 1) * ROWS]
        for block in range(4):
            source = halo_from[owner][block]
            table[owner, ROWS + block * HALO : ROWS + (block + 1) * HALO] = keys[source : source + HALO]
        table[owner, ROWS + 4 * HALO : at_target] = keys[at_coarse : at_coarse + coarse_rows]
        table[owner, at_target : at_target + ROWS] = target[owner * ROWS : (owner + 1) * ROWS]
        table[owner, at_target + ROWS :] = ebuf[...]
        hidden = silu(dot(hot[owner], table[owner])).astype(BF)
        nodes.append(dot(sums[owner], hidden).astype(BF))
    node_in = jnp.concatenate(nodes, axis=0)
    second[0].wait()
    kept = dot(old, wbuf[3])
    second[1].wait()

    def vector(at):
        return (ebuf[at : at + 1].astype(F32) + ebuf[at + 1 : at + 2].astype(F32)) + ebuf[
            at + 2 : at + 3
        ].astype(F32)

    update = silu(dot(node_in, wbuf[2]) + kept + vector(NODE_BIAS))
    new = (old.astype(F32) + layer_norm(update, vector(GAIN))).astype(BF)
    if last:
        rows = jnp.where(core_index() == 0, new[:ROWS], new[ROWS:])
        outs[0][...] = dot(rows, tail_weight[0]).astype(BF)
    else:
        outs[0][...] = new
        outgoing(new, tail_weight, *outs[1:])


def deliver_kernel(keys, senders, own, near, far):
    both = jnp.concatenate([keys[0], keys[1]], axis=0)
    send_blocks(both, senders, own, near, far)


def decode_kernel(own, near, far, queries, features, weight, bias, receivers, x, out_weight, out):
    edge = edge_term(feature_rows(features), weight[...]) + bias[...]
    hot = hot_rows(receivers[...], ROWS)
    width = out_weight.shape[0]
    for sample in range(2):
        at = pl.ds(sample * ROWS, ROWS)
        rows = arrived_rows(own, near, far, sample)
        hidden = silu(rows + dot_t(hot, queries[at]) + edge).astype(BF)
        total = dot(hot, hidden).astype(BF)
        change = lax.dot_general(
            total, out_weight[...], (((1,), (1,)), ((), ())), preferred_element_type=F32
        )
        out[sample] = (x[at, :width].astype(F32) + change).astype(BF)


def shards(
    grid_inputs, embed_weight, embed_bias, encode_weight, encode_edge_weight, encode_bias, mesh_gain,
    process_weight, process_edge_weight, process_bias, process_gain, decode_weight, decode_edge_weight,
    decode_bias, output_weight, encode_senders, encode_receivers, encode_features, halo_send_rows,
    mesh_senders, mesh_receivers, mesh_features, decode_senders, decode_receivers, decode_features,
):
    samples, grid_rows, in_width = grid_inputs.shape
    latent = embed_weight.shape[1]
    owners = lax.axis_size("space")
    chips = owners // 2
    sections = lax.axis_size("section")
    core_id = lax.axis_index("space") % 2
    pairs = [[2 * k, 2 * k + 1] for k in range(chips)]
    same_core = [[2 * k + c for k in range(chips)] for c in range(2)]
    crossings = [[2 * k + 1, (2 * k + 2) % owners] for k in range(chips)]
    swap = [(i, i ^ 1) for i in range(owners)]

    def gather_pair(value):
        return lax.all_gather(value, "space", axis=0, axis_index_groups=pairs)

    def gather_crossing(value):
        return lax.all_gather(value, "space", axis=0, axis_index_groups=crossings)

    def vec(value):
        return value.reshape(1, -1)

    half_rows = 2 * latent + EXTRA
    half = call(
        pack_weights_kernel,
        shape((half_rows, latent)),
        process_edge_weight[0], process_bias[0], process_gain, process_weight[0],
        hbm=4, hbm_out=True, limit=PACK_LIMIT,
        scratch=[
            pltpu.VMEM(process_edge_weight.shape[1:], F32),
            pltpu.VMEM(process_bias.shape[1:], F32),
            pltpu.VMEM(process_gain.shape, F32),
            pltpu.VMEM((half_rows, latent), BF),
            pltpu.SemaphoreType.DMA((12,)),
        ],
    )
    gathered = lax.all_gather(half, "section", axis=0)

    grid_inputs, half = lax.optimization_barrier((grid_inputs, half))
    x = grid_inputs.reshape(samples * grid_rows, in_width)
    cap = encode_senders.shape[2] // 3
    block = shape((samples * cap, latent))
    own, near, far, queries = call(
        embed_kernel,
        (block, block, block, shape((samples * grid_rows, latent))),
        x, embed_weight, vec(embed_bias), encode_weight, decode_weight, encode_senders[0],
    )
    far = gather_crossing(far)
    near = gather_pair(near)
    edges = mesh_senders.shape[1]
    b = halo_send_rows.reshape(4, HALO)
    none = jnp.zeros((HALO,), jnp.int32)
    low = jnp.concatenate([b[2], none, none, b[1], b[3], none, none, b[0]])
    high = jnp.concatenate([none, b[0] + ROWS, b[2] + ROWS, none, none, b[3] + ROWS, b[1] + ROWS, none])
    halo_list = jnp.pad(jnp.where(core_id == 0, low, high), (0, edges - 8 * HALO))
    meta = jnp.concatenate(
        [
            jnp.stack([mesh_senders[0], mesh_receivers[0], halo_list, jnp.zeros_like(halo_list)]).astype(F32),
            mesh_features[:, 0, :],
        ],
        axis=0,
    )
    meta = gather_pair(meta)
    table_rows = 2 * ROWS + 4 * HALO + owners + EXTRA
    edges_hot, sums_hot, halo_hot = call(
        functools.partial(setup_kernel, coarse=owners),
        (shape((2, edges, table_rows)), shape((2, ROWS, edges)), shape((8 * HALO, 2 * ROWS))),
        meta,
    )
    parts = call(
        message_kernel,
        shape((sections, ROWS, latent)),
        own, near, far, encode_features[:, 0], encode_edge_weight, vec(encode_bias), encode_receivers[0],
    )
    parts = lax.all_to_all(parts, "section", 0, 0, tiled=True)
    start = call(start_kernel, shape((ROWS, latent)), parts, vec(mesh_gain))
    state = gather_pair(start).reshape(2 * ROWS, latent)

    outgoing_shapes = (
        shape((chips, 2, latent)),
        shape((3 * HALO, latent)),
        shape((2 * HALO, latent)),
    )
    scratch = [
        pltpu.VMEM((4, latent, latent), BF),
        pltpu.VMEM((EXTRA, latent), BF),
        pltpu.VMEM((2 * ROWS + 8 * HALO + owners, latent), BF),
        pltpu.VMEM((2, table_rows, latent), BF),
        pltpu.SemaphoreType.DMA((5,)),
    ]
    coarse, halo, inner = call(prepare_kernel, outgoing_shapes, state, halo_hot)
    for layer in range(4):
        coarse = lax.all_to_all(coarse, "space", 0, 0, tiled=True, axis_index_groups=same_core)
        coarse = coarse.reshape(owners, latent)
        halo = gather_pair(gather_crossing(halo))
        if layer == 0:
            gathered, halo, coarse = lax.optimization_barrier((gathered, halo, coarse))
            gathered_other = lax.ppermute(gathered[0], "space", swap)
        last = layer == 3
        tail = decode_weight if last else halo_hot
        weights = (gathered, gathered_other)
        inputs = (state, halo, inner, coarse, edges_hot, sums_hot, tail) + weights
        if last:
            out = (shape((ROWS, latent)),)
        else:
            out = (shape(state.shape),) + outgoing_shapes
        out = call(
            functools.partial(layer_kernel, layer=layer, last=last),
            out, *inputs,
            hbm=2, limit=FIRST_LIMIT if layer == 0 else LAYER_LIMIT, scratch=scratch,
        )
        if last:
            keys = out[0]
        else:
            state, coarse, halo, inner = out
        if layer == 0:
            gathered, state = lax.optimization_barrier((gathered, state))
            gathered_other = lax.ppermute(gathered, "space", swap)

    twins = [[i, i + 1] for i in range(0, sections, 2)]
    keys = lax.all_gather(keys, "section", axis=0, axis_index_groups=twins)
    own, near, far = call(deliver_kernel, (block, block, block), keys, decode_senders[0])
    far = gather_crossing(far)
    near = gather_pair(near)
    return call(
        decode_kernel,
        shape((samples, grid_rows, output_weight.shape[1])),
        own, near, far, queries, decode_features[:, 0], decode_edge_weight, vec(decode_bias),
        decode_receivers[0], x, output_weight.T,
    )


def solution(mesh):
    return jax.shard_map(
        shards,
        mesh=mesh,
        in_specs=(
            P(None, ("section", "space"), None),
            P(),
            P(),
            P(),
            P(),
            P(),
            P(),
            P("section", None, None, None),
            P("section", None, None),
            P("section", None, None),
            P("section", None),
            P(),
            P(),
            P(),
            P(),
            P("section", "space", None),
            P("section", "space", None),
            P(None, "section", "space", None),
            P("space", None),
            P("space", None),
            P("space", None),
            P(None, "space", None),
            P("section", "space", None),
            P("section", "space", None),
            P(None, "section", "space", None),
        ),
        out_specs=P(None, ("section", "space"), None),
        check_vma=False,
    )
```
